256 devices in a mesh: seq: 8 (over y, z_lo), res: 32 (over z_hi, x, core).
Axes of the slice: x: 4, y: 4, z: 8 (z_hi: 4, z_lo: 2; z = z_hi * 2 + z_lo), core: 2. Of those that a mesh axis runs over, the one named last changes fastest.
Arguments:
- homolog_stack: bfloat16 [256, 512, 256], P('seq', 'res'), may hold values from -6 to 6
- presence_flags: int32 [256, 512], P('seq', 'res'), may hold values from 0 to 1, as said below
- normalizer_scaling: float32 [256], replicated, may hold values from 0.25 to 1.75
- normalizer_offset: float32 [256], replicated, may hold values from -1.5 to 1.5
- first_factor_matrix: bfloat16 [256, 32], replicated, may hold values from -0.375 to 0.375
- first_factor_offset: float32 [32], replicated, may hold values from -2.5 to 2.5
- second_factor_matrix: bfloat16 [256, 32], replicated, may hold values from -0.375 to 0.375
- second_factor_offset: float32 [32], replicated, may hold values from -2.5 to 2.5
- final_mapping_matrix: bfloat16 [1024, 128], replicated, may hold values from -2.5 to 2.5
- coupling_delta_cotangent: bfloat16 [512, 512, 128], P('res', 'seq'), may hold values from -6 to 6
Outputs:
- pair: bfloat16 [512, 512, 128], P('res', 'seq')
- alignment_gradient: bfloat16 [256, 512, 256], P('seq', 'res')
The draws below stay inside these ranges and needn't reach their ends.
Inputs may be any that keep to these rules, and one draw needn't show every extreme that they name: Row 0 of presence_flags (the target sequence) is all ones.
All inputs are finite; a program needn't handle non-finite values.
Results may differ from the reference program's by a relative error of at most 0.017.
Values may be sent and summed in bfloat16 or wider, within the bound.
A program may use at most 64 MiB of HBM per device.

```python
import jax
import jax.numpy as jnp
from jax import lax

ROW_WIDTH = 256
HIDDEN_WIDTH = 32
COUPLING_WIDTH = 128
LOCAL_SPAN = 16
HOMOLOG_COUNT = 256
WINDOW_LENGTH = 512


def draw_presence_flags(key, part):
    key = jax.random.fold_in(key, 11)
    key_cols, random_shifts = jax.random.split(key)
    matrix_lines = lax.broadcasted_iota(jnp.int32, (HOMOLOG_COUNT, WINDOW_LENGTH), 0)
    tier_index = 300 + 600 * matrix_lines // HOMOLOG_COUNT
    column = jax.random.randint(key_cols, (1, WINDOW_LENGTH), 60, 101, dtype=jnp.int32)
    threshold = tier_index * column // 100
    cyclic_shifts = jax.random.randint(random_shifts, (HOMOLOG_COUNT, WINDOW_LENGTH), 0, 1000, dtype=jnp.int32)
    present = jnp.where(cyclic_shifts < threshold, 1, 0).astype(jnp.int32)
    return jnp.where(matrix_lines == 0, 1, present).astype(jnp.int32)


def strengthened(result, stream_key, source, target, blocks, factor):
    owner, partner = [(jnp.arange(result.shape[position]) // (result.shape[position] // blocks)).reshape([-1 if axis == position else 1 for axis in range(result.ndim)]) for position in (source, target)]
    chosen = jax.random.permutation(stream_key, blocks)[partner]
    strong = (owner == chosen) | (owner == (partner + blocks // 2) % blocks)
    return jnp.where(strong, factor * result, result)


def levels(rng, dims, cuts, least, largest):
    factor_of = 1.0
    for position, shards_of in cuts:
        heights = jax.random.uniform(jax.random.fold_in(jax.random.fold_in(rng, 6), position), (shards_of,), jnp.float32, least / len(cuts), largest / len(cuts))
        factor_of = factor_of * jnp.repeat(jnp.exp(heights), dims[position] // shards_of).reshape((-1,) + (1,) * (len(dims) - 1 - position))
    return factor_of


def noise(stream_key, extent, scale, most, cuts=(), kind=jnp.bfloat16):
    array = scale * jax.random.normal(stream_key, extent, jnp.float32)
    if cuts:
        array = array * levels(stream_key, extent, cuts, -0.22, 0.18)
    return jnp.clip(array, -most, most).astype(kind)


def bell_draw_with(key, dims, scale, most, pieces, heavy, held_as=jnp.bfloat16):
    result = scale * jax.random.normal(key, dims, jnp.float32)
    if pieces:
        result = result * levels(key, dims, pieces, -0.22, 0.18)
    return jnp.clip(strengthened(result, jax.random.fold_in(key, 3), *heavy), -most, most).astype(held_as)


def setup_inputs(seed: int = 0) -> dict:
    keys = jax.random.split(jax.random.key(seed), 11)
    return {
        "homolog_stack": noise(keys[0], (HOMOLOG_COUNT, WINDOW_LENGTH, ROW_WIDTH), 1.0, 6.0, ((0, 8), (1, 32))),
        "presence_flags": draw_presence_flags(jax.random.fold_in(keys[10], 71), 0),
        "normalizer_scaling": jnp.clip(1.0 + 0.15 * jax.random.normal(keys[2], (ROW_WIDTH,), jnp.float32), 0.25, 1.75),
        "normalizer_offset": noise(keys[3], (ROW_WIDTH,), 0.3, 1.5, (), jnp.float32),
        "first_factor_matrix": noise(keys[4], (ROW_WIDTH, HIDDEN_WIDTH), ROW_WIDTH ** -0.5, 0.375),
        "first_factor_offset": noise(keys[5], (HIDDEN_WIDTH,), 0.5, 2.5, (), jnp.float32),
        "second_factor_matrix": noise(keys[6], (ROW_WIDTH, HIDDEN_WIDTH), ROW_WIDTH ** -0.5, 0.375),
        "second_factor_offset": noise(keys[7], (HIDDEN_WIDTH,), 0.5, 2.5, (), jnp.float32),
        "final_mapping_matrix": noise(keys[8], (HIDDEN_WIDTH * HIDDEN_WIDTH, COUPLING_WIDTH), (max(1, 1600 // HOMOLOG_COUNT)) ** -0.5, 2.5),
        "coupling_delta_cotangent": bell_draw_with(keys[9], (WINDOW_LENGTH, WINDOW_LENGTH, COUPLING_WIDTH), 1.0, 6.0, ((0, 32), (1, 8)), (0, 1, 32, 2.75)),
    }


def homolog_embedding(homolog_cells, flag_cells, normalizer_scaling, normalizer_offset, first_factor_matrix, first_factor_offset, second_factor_matrix, second_factor_offset):
    middle_product = lax.optimization_barrier(jnp.mean(homolog_cells, axis=-1, keepdims=True))
    mean_removed = homolog_cells - middle_product
    spread = lax.optimization_barrier(jnp.mean(mean_removed * mean_removed, axis=-1, keepdims=True))
    normed = mean_removed * lax.rsqrt(spread + 1e-05) * normalizer_scaling + normalizer_offset
    first_factor_hidden = jnp.einsum('sic,cd->sid', normed, first_factor_matrix.astype(jnp.float32), precision=lax.Precision.HIGHEST) + first_factor_offset
    second_factor_hidden = jnp.einsum('sic,cd->sid', normed, second_factor_matrix.astype(jnp.float32), precision=lax.Precision.HIGHEST) + second_factor_offset
    return (flag_cells[:, :, None] * first_factor_hidden, flag_cells[:, :, None] * second_factor_hidden)

def reference(homolog_stack, presence_flags, normalizer_scaling, normalizer_offset, first_factor_matrix, first_factor_offset, second_factor_matrix, second_factor_offset, final_mapping_matrix, coupling_delta_cotangent):
    flag_cells = presence_flags.astype(jnp.float32)

    def widened_source(numeric_array):
        return homolog_embedding(numeric_array, flag_cells, normalizer_scaling, normalizer_offset, first_factor_matrix, first_factor_offset, second_factor_matrix, second_factor_offset)
    (first_factor_hidden, second_factor_hidden), reverse_rule = jax.vjp(widened_source, homolog_stack.astype(jnp.float32))
    left_t = jnp.transpose(first_factor_hidden.astype(jnp.bfloat16), (1, 0, 2))
    second_factor_lines = jnp.transpose(second_factor_hidden.astype(jnp.bfloat16), (1, 0, 2)).reshape(WINDOW_LENGTH, HOMOLOG_COUNT * HIDDEN_WIDTH)
    second_factor_lines = lax.optimization_barrier(second_factor_lines).astype(jnp.float32)
    flattened_matrix = final_mapping_matrix.astype(jnp.float32).reshape(HIDDEN_WIDTH, HIDDEN_WIDTH * COUPLING_WIDTH)
    counts = jnp.dot(flag_cells.T, flag_cells, precision=lax.Precision.HIGHEST)
    denom = counts + 0.001
    scaled = (coupling_delta_cotangent.astype(jnp.float32) / denom[:, :, None]).astype(jnp.bfloat16)
    scaled = lax.optimization_barrier(scaled).astype(jnp.float32)

    def loop_counter(carry, index):
        start = (index * LOCAL_SPAN).astype(jnp.int32)
        left_blk = lax.dynamic_slice_in_dim(left_t, start, LOCAL_SPAN, 0).astype(jnp.float32)
        collapsed_sum = jnp.einsum('isc,cq->isq', left_blk, flattened_matrix).astype(jnp.bfloat16)
        collapsed_sum = lax.optimization_barrier(collapsed_sum).astype(jnp.float32).reshape(LOCAL_SPAN, HOMOLOG_COUNT * HIDDEN_WIDTH, COUPLING_WIDTH)
        numer = jnp.einsum('jp,ipk->ijk', second_factor_lines, collapsed_sum)
        den_blk = lax.dynamic_slice_in_dim(denom, start, LOCAL_SPAN, 0)
        pair_blk = (numer / den_blk[:, :, None]).astype(jnp.bfloat16)
        scaled_blk = lax.dynamic_slice_in_dim(scaled, start, LOCAL_SPAN, 0)
        traversed_state = jnp.einsum('jp,ijk->ipk', second_factor_lines, scaled_blk).astype(jnp.bfloat16)
        traversed_state = lax.optimization_barrier(traversed_state).astype(jnp.float32)
        first_factor_cotangent_value = jnp.einsum('nlw,ow->nlo', traversed_state.reshape(LOCAL_SPAN, HOMOLOG_COUNT, HIDDEN_WIDTH * COUPLING_WIDTH), flattened_matrix)
        right_part = jnp.einsum('ijk,ipk->jp', scaled_blk, collapsed_sum)
        return (carry + right_part, (pair_blk, first_factor_cotangent_value))
    accumulated_sum, (couplings, first_factor_cotangent_list) = lax.scan(loop_counter, jnp.zeros((WINDOW_LENGTH, HOMOLOG_COUNT * HIDDEN_WIDTH), jnp.float32), jnp.arange(WINDOW_LENGTH // LOCAL_SPAN, dtype=jnp.int32))
    pair = couplings.reshape(WINDOW_LENGTH, WINDOW_LENGTH, COUPLING_WIDTH)
    first_factor_cotangent_value = jnp.transpose(first_factor_cotangent_list.reshape(WINDOW_LENGTH, HOMOLOG_COUNT, HIDDEN_WIDTH), (1, 0, 2))
    second_factor_cotangent_value = jnp.transpose(accumulated_sum.reshape(WINDOW_LENGTH, HOMOLOG_COUNT, HIDDEN_WIDTH), (1, 0, 2))
    alignment_gradient = reverse_rule((first_factor_cotangent_value, second_factor_cotangent_value))[0]
    return (pair, alignment_gradient.astype(jnp.bfloat16))
```

```python
import jax
import jax.numpy as jnp
from jax import lax
from jax.experimental import pallas as pl
from jax.experimental.pallas import tpu as pltpu
from jax.sharding import PartitionSpec as P

F32 = jnp.float32
BF = jnp.bfloat16
MESH = pl.DeviceIdType.MESH


def dot(a, b, ca=1, cb=0):
    return lax.dot_general(a, b, (((ca,), (cb,)), ((), ())), preferred_element_type=F32)


def rem(a, n):
    return lax.rem(a, jnp.int32(n))


def div(a, n):
    return lax.div(a, jnp.int32(n))


def split(a):
    hi = a.astype(BF)
    return hi, (a - hi.astype(F32)).astype(BF)


def ones_where(condition):
    return jnp.where(condition, 1.0, 0.0)


def iota(shape, dim):
    return lax.broadcasted_iota(jnp.int32, shape, dim)


def swap_halves(a, b):
    low = iota(a.shape, 1) < 64
    return (
        jnp.where(low, a, pltpu.roll(b, 64, 1)),
        jnp.where(low, pltpu.roll(a, 64, 1), b),
    )


def kernel(
    x_ref, flag_ref, gain_ref, shift_ref, w1_ref, b1_ref, w2_ref, b2_ref, wm_ref, delta_ref,
    pair_ref, grad_ref,
    xhat_ref, rstd_ref, proj_ref, wf_ref, wec_ref, wt_ref, dt_ref, mask1_ref, mask2_ref, perm1_ref, perm2_ref,
    zbuf, lall, rall, left_ref, right_ref, tile_ref, d_ref, pt_ref,
    gsend, gcore, hsend, gx, ksend, gy, gz, lsend, lrecv, dn_ref,
    zs, zr, ys, yr, xs, xr, cs, cr, ls, lr,
    bzs, bzr, bys, byr, bxs, bxr, bcs, bcr, bls, blr,
):
    q = lax.axis_index("seq")
    r = lax.axis_index("res")
    y, zl = div(q, 2), rem(q, 2)
    zh, x, core = div(r, 8), rem(div(r, 2), 4), rem(r, 2)
    other = 1 - core

    def device(x_=x, y_=y, zh_=zh, zl_=zl, core_=core):
        return {"seq": y_ * 2 + zl_, "res": zh_ * 8 + x_ * 2 + core_}

    def crossed(x_):
        return rem(div(x_, 2) + zl, 2)

    def twin(x_):
        m = crossed(x_)
        return x_ + m * (3 - 2 * x_), rem(zl + m, 2)

    mine_crossed = crossed(x)
    tx, tzl = twin(x)

    def remote(src, dst, send, recv, where):
        return pltpu.make_async_remote_copy(
            src_ref=src, dst_ref=dst, send_sem=send, recv_sem=recv, device_id=where, device_id_type=MESH
        )

    barrier = pltpu.get_barrier_semaphore()

    def greet(where):
        pl.semaphore_signal(barrier, inc=1, device_id=where, device_id_type=MESH)

    for d in range(1, 4):
        greet(device(zh_=rem(zh + d, 4)))
        greet(device(x_=rem(x + d, 4)))
    greet(device(core_=other))
    for k in range(1, 8):
        greet(device(y_=rem(y + k // 2, 4), zl_=rem(zl + k % 2, 2)))

    @pl.when(mine_crossed == 1)
    def _():
        for t in range(4):
            greet(device(x_=tx, zl_=tzl, y_=jnp.int32(t)))

    xv = x_ref[...].astype(F32).reshape(512, 256)
    centred = xv - jnp.mean(xv, axis=-1, keepdims=True)
    rstd = lax.rsqrt(jnp.mean(centred * centred, axis=-1, keepdims=True) + 1e-5)
    xhat = centred * rstd
    xhat_ref[...] = xhat
    rstd_ref[...] = jnp.broadcast_to(rstd, (512, 128))
    hi, lo = split(xhat * gain_ref[...] + shift_ref[...])
    w = jnp.concatenate([w1_ref[...], w2_ref[...]], axis=1)
    bias = jnp.concatenate([b1_ref[...], b2_ref[...]], axis=1)
    proj_ref[:, 0:64] = dot(hi, w) + dot(lo, w) + bias

    rows, cols = iota((512, 512), 0), iota((512, 512), 1)
    perm1 = ones_where(((rows >> 5) == (cols & 15)) & ((rows & 31) == (cols >> 4))).astype(BF)
    perm1_ref[...] = perm1
    flags = flag_ref[...].astype(F32).astype(BF)
    mask1 = dot(flags, ones_where(iota((16, 512), 0) == (iota((16, 512), 1) >> 5)).astype(BF))
    mask2 = dot(flags, ones_where(iota((16, 512), 0) == (iota((16, 512), 1) & 15)).astype(BF))
    mask1_ref[...] = mask1
    mask2_ref[...] = mask2
    flags_t = dot(flags, ones_where(iota((32, 128), 0) == iota((32, 128), 1)).astype(BF), 0, 0).astype(BF)
    parts = [proj_ref[pl.ds(i, 32, stride=16), :] for i in range(16)]
    lw = (jnp.concatenate([p[:, 0:32] for p in parts], axis=1) * mask1).astype(BF)
    rw = jnp.concatenate([p[:, 32:64] for p in parts], axis=1).astype(BF)
    rw = (dot(rw, perm1) * mask2).astype(BF)
    for l in range(4):
        for h in range(2):
            lall[zl, y, 2 * l + h] = lw[16 * h : 16 * h + 16, 128 * l : 128 * l + 128]
            zbuf[zh, 2 * l + h] = rw[16 * h : 16 * h + 16, 128 * l : 128 * l + 128]
    lall[zl, y, 8] = flags_t
    zbuf[zh, 8] = flags_t

    pl.semaphore_wait(barrier, 14 + 4 * mine_crossed)

    zcopies = [
        remote(zbuf.at[zh], zbuf.at[zh], zs.at[d - 1], zr.at[d - 1], device(zh_=rem(zh + d, 4))) for d in range(1, 4)
    ]
    for c in zcopies:
        c.start()
    lcopies = [
        remote(
            lall.at[zl, y], lall.at[zl, y], ls.at[k - 1], lr.at[k - 1],
            device(y_=rem(y + k // 2, 4), zl_=rem(zl + k % 2, 2)),
        )
        for k in range(1, 8)
    ]
    for c in lcopies:
        c.start()

    wf_ref[...] = wm_ref[...].astype(F32)
    for e in range(32):
        wec_ref[32 * e : 32 * e + 32, :] = wf_ref[pl.ds(e, 32, stride=32), :].astype(BF)
    wt_ref[...] = wec_ref[...].astype(F32).T.astype(BF)
    dt_ref[...] = delta_ref[...].astype(F32).reshape(1024, 128).T
    perm2_ref[...] = ones_where(
        ((rows >> 7) == ((cols >> 4) & 3)) & (((rows >> 4) & 7) == (cols >> 6)) & ((rows & 15) == (cols & 15))
    ).astype(BF)

    jb = 2 * rem(x, 2) + core
    ycopies = []
    for d in range(4):
        if d:
            zcopies[d - 1].wait_recv()
        t = rem(zh + 4 - d, 4)
        c = remote(zbuf.at[t], rall.at[jb, zl, y], ys.at[d], yr.at[y], device(x_=tx, y_=t, zl_=tzl))
        ycopies.append(c)
        stays = jnp.logical_and(mine_crossed == 0, t == y)

        @pl.when(stays)
        def _(t=t):
            pltpu.make_async_copy(zbuf.at[t], rall.at[jb, zl, y], yr.at[y]).start()

        @pl.when(jnp.logical_not(stays))
        def _(c=c):
            c.start()

    def group(x_, core_):
        gx_, gzl_ = twin(x_)
        return rall.at[2 * rem(gx_, 2) + core_, gzl_]

    own = group(x, core)
    for t in range(4):
        pltpu.make_async_copy(own.at[t], own.at[t], yr.at[t]).wait()
    xcopies = [
        remote(own, own, xs.at[d - 1], xr.at[d - 1], device(x_=rem(x + d, 4))) for d in range(1, 4)
    ]
    for c in xcopies:
        c.start()
    ccopies = []
    for d in range(4):
        g = group(rem(x + 4 - d, 4), core)
        if d:
            xcopies[d - 1].wait_recv()
        c = remote(g, g, cs.at[d], cr.at[d], device(core_=other))
        c.start()
        ccopies.append(c)
    for c in lcopies:
        c.wait_recv()
    left_ref_blocks = [lall[b // 4, b % 4] for b in range(8)]
    for b in range(8):
        for l in range(4):
            for h in range(2):
                left_ref[32 * b + 16 * h : 32 * b + 16 * h + 16, 128 * l : 128 * l + 128] = left_ref_blocks[b][2 * l + h]
    for c in ccopies:
        c.wait_recv()

    mi = jnp.concatenate([lall[b // 4, b % 4, 8] for b in range(8)], axis=1)
    mj = jnp.concatenate(
        [jnp.concatenate([rall[g, b // 4, b % 4, 8] for b in range(8)], axis=1) for g in range(4)], axis=0
    )
    count = dot(mi, mj, 1, 1)
    lane = iota((16, 1024), 1)
    spread = dot(count.astype(BF), ones_where(iota((64, 1024), 0) == (iota((64, 1024), 1) & 63)).astype(BF))
    denom = jnp.sum(jnp.where((lane >> 6) == iota((16, 1024), 0), spread, 0.0), axis=0, keepdims=True) + 0.001
    scaled = (dt_ref[...] / denom).astype(BF)

    for l in range(4):
        packed = jnp.concatenate([rall[g, :, :, 2 * l : 2 * l + 2].reshape(256, 128) for g in range(4)], axis=1)
        right_ref[:, 512 * l : 512 * l + 512] = dot(packed, perm2_ref[...]).astype(BF)

    gcopies = []
    for l in range(4):
        tile_ref[...] = dot(wec_ref[256 * l : 256 * l + 256, :], scaled)

        def spread_pair(p, carry, l=l):
            lanes = pl.ds(pl.multiple_of(p * 128, 128), 128)
            for t in range(4):
                a, b = swap_halves(tile_ref[64 * t : 64 * t + 32, lanes], tile_ref[64 * t + 32 : 64 * t + 64, lanes])
                place = slice(512 * l + 128 * t, 512 * l + 128 * t + 128)
                d_ref[pl.ds(pl.multiple_of(p * 64, 64), 32), place] = a.astype(BF)
                d_ref[pl.ds(pl.multiple_of(p * 64 + 32, 32), 32), place] = b.astype(BF)
            return carry

        lax.fori_loop(0, 8, spread_pair, 0)
        part = dot(left_ref[...], d_ref[:, 512 * l : 512 * l + 512]).astype(BF)
        part = dot(part, perm2_ref[...], 1, 1).astype(BF)
        for g in range(4):
            gsend[l, g % 2, g // 2] = part[:, 128 * g : 128 * g + 128].reshape(2, 4, 2, 16, 128)
        c = remote(gsend.at[l, other], gcore.at[l], bcs.at[l], bcr.at[l], device(core_=other))
        c.start()
        gcopies.append(c)

    part = dot(right_ref[...], d_ref[...], 1, 1)
    lsend[...] = part.astype(BF).reshape(8, 32, 512)
    blcopies = []
    for k in range(1, 8):
        y_, zl_ = rem(y + k // 2, 4), rem(zl + k % 2, 2)
        c = remote(lsend.at[zl_ * 4 + y_], lrecv.at[k - 1], bls.at[k - 1], blr.at[k - 1], device(y_=y_, zl_=zl_))
        c.start()
        blcopies.append(c)

    bxcopies = []
    for l in range(4):
        gcopies[l].wait_recv()
        hsend[l] = (gsend[l, core].astype(F32) + gcore[l].astype(F32)).astype(BF)
        for d in range(1, 4):
            x_ = rem(x + d, 4)
            gx_, gzl_ = twin(x_)
            c = remote(
                hsend.at[l, rem(gx_, 2), gzl_], gx.at[l, d - 1], bxs.at[l, d - 1], bxr.at[l, d - 1], device(x_=x_)
            )
            c.start()
            bxcopies.append(c)

    def pair_part(l):
        o = dot(left_ref[...], right_ref[:, 512 * l : 512 * l + 512], 0, 0)
        for t in range(4):
            for p in range(8):
                a, b = swap_halves(
                    o[64 * p : 64 * p + 32, 128 * t : 128 * t + 128],
                    o[64 * p + 32 : 64 * p + 64, 128 * t : 128 * t + 128],
                )
                tile_ref[64 * t : 64 * t + 32, 128 * p : 128 * p + 128] = a
                tile_ref[64 * t + 32 : 64 * t + 64, 128 * p : 128 * p + 128] = b
        term = dot(wt_ref[:, 256 * l : 256 * l + 256], tile_ref[...].astype(BF))
        if l == 0:
            pt_ref[...] = term
        else:
            pt_ref[...] += term

    for l in range(4):
        pair_part(l)

    for l in range(4):
        for d in range(3):
            bxcopies[3 * l + d].wait_recv()
        total = hsend[l, rem(tx, 2), tzl].astype(F32)
        for d in range(3):
            total = total + gx[l, d].astype(F32)
        ksend[:, 2 * l : 2 * l + 2] = total.astype(BF)

    bycopies = []
    for d in range(4):
        t = rem(y + d, 4)
        c = remote(ksend.at[t], gy.at[y], bys.at[d], byr.at[y], device(x_=tx, y_=t, zl_=tzl))
        bycopies.append(c)
        if d == 0:

            @pl.when(mine_crossed == 0)
            def _():
                pltpu.make_async_copy(ksend.at[y], gy.at[y], byr.at[y]).start()

            @pl.when(mine_crossed == 1)
            def _(c=c):
                c.start()
        else:
            c.start()

    pair_ref[...] = (pt_ref[...] / denom).T.astype(BF).reshape(16, 64, 128)

    for c in blcopies:
        c.wait_recv()
    dl = lsend[zl * 4 + y].astype(F32)
    for k in range(7):
        dl = dl + lrecv[k].astype(F32)
    dl = dl * mask1_ref[...]

    for t in range(4):
        pltpu.make_async_copy(gy.at[t], gy.at[t], byr.at[t]).wait()
    bzcopies = []
    for d in range(1, 4):
        t = rem(zh + d, 4)
        c = remote(gy.at[t], gz.at[d - 1], bzs.at[d - 1], bzr.at[d - 1], device(zh_=t))
        c.start()
        bzcopies.append(c)
    for c in bzcopies:
        c.wait_recv()
    total = gy[zh].astype(F32)
    for d in range(3):
        total = total + gz[d].astype(F32)
    dr = jnp.concatenate(
        [jnp.concatenate([total[2 * l], total[2 * l + 1]], axis=0) for l in range(4)], axis=1
    ) * mask2_ref[...]
    hi, lo = split(dr)
    dr = dot(hi, perm1_ref[...], 1, 1) + dot(lo, perm1_ref[...], 1, 1)

    rows_i = jnp.concatenate(
        [
            jnp.concatenate([dl[:, 32 * i : 32 * i + 32], dr[:, 32 * i : 32 * i + 32]], axis=1)
            for i in range(16)
        ],
        axis=0,
    )
    hi, lo = split(rows_i)
    w = jnp.concatenate([w1_ref[...], w2_ref[...]], axis=1)
    dn = dot(hi, w, 1, 1) + dot(lo, w, 1, 1)
    for i in range(16):
        for h in range(2):
            dn_ref[h, pl.ds(i, 32, stride=16), :] = dn[32 * i : 32 * i + 32, 128 * h : 128 * h + 128]
    dn = jnp.concatenate([dn_ref[0], dn_ref[1]], axis=1) * gain_ref[...]
    xhat = xhat_ref[...]
    dx = rstd_ref[:, 0:1] * (
        dn - jnp.mean(dn, axis=-1, keepdims=True) - xhat * jnp.mean(dn * xhat, axis=-1, keepdims=True)
    )
    grad_ref[...] = dx.astype(BF).reshape(32, 16, 256)

    for c in zcopies + lcopies + xcopies + ccopies + gcopies + blcopies + bxcopies + bzcopies:
        c.wait_send()
    for d in range(4):
        t = rem(zh + 4 - d, 4)

        @pl.when(jnp.logical_not(jnp.logical_and(mine_crossed == 0, t == y)))
        def _(c=ycopies[d]):
            c.wait_send()

    @pl.when(mine_crossed == 1)
    def _():
        bycopies[0].wait_send()

    for c in bycopies[1:]:
        c.wait_send()


def body(
    homolog_stack,
    presence_flags,
    normalizer_scaling,
    normalizer_offset,
    first_factor_matrix,
    first_factor_offset,
    second_factor_matrix,
    second_factor_offset,
    final_mapping_matrix,
    coupling_delta_cotangent,
):
    dma = pltpu.SemaphoreType.DMA
    vm = pltpu.VMEM
    whole = pl.BlockSpec(memory_space=pltpu.VMEM)
    return tuple(
        pl.pallas_call(
            kernel,
            out_shape=(
                jax.ShapeDtypeStruct((16, 64, 128), BF),
                jax.ShapeDtypeStruct((32, 16, 256), BF),
            ),
            in_specs=[whole] * 10,
            out_specs=(whole, whole),
            scratch_shapes=[
                vm((512, 256), F32),
                vm((512, 128), F32),
                vm((512, 128), F32),
                vm((1024, 128), F32),
                vm((1024, 128), BF),
                vm((128, 1024), BF),
                vm((128, 1024), F32),
                vm((32, 512), F32),
                vm((32, 512), F32),
                vm((512, 512), BF),
                vm((512, 512), BF),
                vm((4, 9, 16, 128), BF),
                vm((2, 4, 9, 16, 128), BF),
                vm((4, 2, 4, 9, 16, 128), BF),
                vm((256, 512), BF),
                vm((256, 2048), BF),
                vm((256, 1024), F32),
                vm((512, 2048), BF),
                vm((128, 1024), F32),
                vm((4, 2, 2, 2, 4, 2, 16, 128), BF),
                vm((4, 2, 2, 4, 2, 16, 128), BF),
                vm((4, 2, 2, 4, 2, 16, 128), BF),
                vm((4, 3, 4, 2, 16, 128), BF),
                vm((4, 8, 16, 128), BF),
                vm((4, 8, 16, 128), BF),
                vm((3, 8, 16, 128), BF),
                vm((8, 32, 512), BF),
                vm((7, 32, 512), BF),
                vm((2, 512, 128), F32),
                dma((3,)), dma((3,)),
                dma((4,)), dma((4,)),
                dma((3,)), dma((3,)),
                dma((4,)), dma((4,)),
                dma((7,)), dma((7,)),
                dma((3,)), dma((3,)),
                dma((4,)), dma((4,)),
                dma((4, 3)), dma((4, 3)),
                dma((4,)), dma((4,)),
                dma((7,)), dma((7,)),
            ],
            compiler_params=pltpu.CompilerParams(
                collective_id=0, has_side_effects=True, vmem_limit_bytes=48 * 1024 * 1024
            ),
        )(
            homolog_stack,
            presence_flags,
            normalizer_scaling.reshape(1, 256),
            normalizer_offset.reshape(1, 256),
            first_factor_matrix,
            first_factor_offset.reshape(1, 32),
            second_factor_matrix,
            second_factor_offset.reshape(1, 32),
            final_mapping_matrix,
            coupling_delta_cotangent,
        )
    )


def solution(mesh):
    return jax.shard_map(
        body,
        mesh=mesh,
        in_specs=(
            P("seq", "res", None),
            P("seq", "res"),
            P(),
            P(),
            P(),
            P(),
            P(),
            P(),
            P(),
            P("res", "seq", None),
        ),
        out_specs=(P("res", "seq", None), P("seq", "res", None)),
        check_vma=False,
    )
```

```python
import jax
import jax.numpy as jnp
from jax import lax
from jax.experimental import pallas as pl
from jax.experimental.pallas import tpu as pltpu
from jax.sharding import PartitionSpec as P

F32 = jnp.float32
BF = jnp.bfloat16
MESH = pl.DeviceIdType.MESH


def dot(a, b, ca=1, cb=0):
    return lax.dot_general(a, b, (((ca,), (cb,)), ((), ())), preferred_element_type=F32)


def rem(a, n):
    return lax.rem(a, jnp.int32(n))


def div(a, n):
    return lax.div(a, jnp.int32(n))


def split(a):
    hi = a.astype(BF)
    return hi, (a - hi.astype(F32)).astype(BF)


def ones_where(condition):
    return jnp.where(condition, 1.0, 0.0)


def iota(shape, dim):
    return lax.broadcasted_iota(jnp.int32, shape, dim)


def swap_halves(a, b):
    low = iota(a.shape, 1) < 64
    return (
        jnp.where(low, a, pltpu.roll(b, 64, 1)),
        jnp.where(low, pltpu.roll(a, 64, 1), b),
    )


NEAR = ((0, 0), (0, 1), (0, 3), (1, 0), (3, 0), (1, 1), (1, 3), (3, 1), (3, 3), (0, 2), (2, 0), (1, 2), (3, 2), (2, 1), (2, 3), (2, 2))


def kernel(
    x_hbm, flag_hbm, gain_hbm, shift_hbm, w1_hbm, b1_hbm, w2_hbm, b2_hbm, wm_hbm, delta_hbm,
    pair_ref, grad_ref,
    x_ref, flag_ref, gain_ref, shift_ref, w1_ref, b1_ref, w2_ref, b2_ref, wm_ref, delta_ref, in_sem,
    xhat_ref, rstd_ref, proj_ref, wf_ref, wec_ref, wt_ref, dt_ref, mask1_ref, mask2_ref, perm1_ref, perm2_ref,
    wire, zbuf, lall, rall, left_ref, right_ref, tile_ref, d_ref, rec_ref, pt_ref,
    gsend, gcore, hsend, gx, ksend, gz, lsend, lrecv, dn_ref,
    zs, zr, bs, br, cs, cr, ls, lr,
    gcs, gcr, gbs, gbr, gzs, gzr, gls, glr,
):
    inputs = [
        pltpu.make_async_copy(a, b, in_sem.at[n])
        for n, (a, b) in enumerate(
            zip(
                (x_hbm, flag_hbm, gain_hbm, shift_hbm, w1_hbm, b1_hbm, w2_hbm, b2_hbm, wm_hbm, delta_hbm),
                (x_ref, flag_ref, gain_ref, shift_ref, w1_ref, b1_ref, w2_ref, b2_ref, wm_ref, delta_ref),
            )
        )
    ]
    for c in inputs:
        c.start()

    q = lax.axis_index("seq")
    r = lax.axis_index("res")
    y, zl = div(q, 2), rem(q, 2)
    zh, x, core = div(r, 8), rem(div(r, 2), 4), rem(r, 2)
    other = 1 - core

    def device(x_=x, y_=y, zh_=zh, zl_=zl, core_=core):
        return {"seq": y_ * 2 + zl_, "res": zh_ * 8 + x_ * 2 + core_}

    def twin(x_):
        m = rem(div(x_, 2) + zl, 2)
        return x_ + m * (3 - 2 * x_), rem(zl + m, 2)

    crossed = rem(div(x, 2) + zl, 2)
    tx, tzl = twin(x)

    def remote(src, dst, send, recv, where):
        return pltpu.make_async_remote_copy(
            src_ref=src, dst_ref=dst, send_sem=send, recv_sem=recv, device_id=where, device_id_type=MESH
        )

    def landed(ref, sem):
        pltpu.make_async_copy(ref, ref, sem).wait()

    barrier = pltpu.get_barrier_semaphore()

    def greet(where):
        pl.semaphore_signal(barrier, inc=1, device_id=where, device_id_type=MESH)

    for d in (2, 1, 3):
        greet(device(x_=tx, zl_=tzl, zh_=rem(zh + d, 4)))

    @pl.when(crossed == 1)
    def _():
        greet(device(x_=tx, zl_=tzl))

    for dx, dy in NEAR[1:]:
        greet(device(x_=rem(x + dx, 4), y_=rem(y + dy, 4)))
    for dy in range(4):
        greet(device(y_=rem(y + dy, 4), zl_=1 - zl))
    greet(device(core_=other))

    rows, cols = iota((512, 512), 0), iota((512, 512), 1)
    perm1 = ones_where(((rows >> 5) == (cols & 15)) & ((rows & 31) == (cols >> 4))).astype(BF)
    perm1_ref[...] = perm1
    for c in inputs[:8]:
        c.wait()
    xv = x_ref[...].astype(F32).reshape(512, 256)
    centred = xv - jnp.mean(xv, axis=-1, keepdims=True)
    rstd = lax.rsqrt(jnp.mean(centred * centred, axis=-1, keepdims=True) + 1e-5)
    xhat = centred * rstd
    xhat_ref[...] = xhat
    rstd_ref[...] = jnp.broadcast_to(rstd, (512, 128))
    hi, lo = split(xhat * gain_ref[...] + shift_ref[...])
    w = jnp.concatenate([w1_ref[...], w2_ref[...]], axis=0)
    bias = jnp.concatenate([b1_ref[...], b2_ref[...]], axis=1)
    proj_ref[:, 0:64] = dot(hi, w, 1, 1) + dot(lo, w, 1, 1) + bias

    flags_t = flag_ref[...].astype(F32).astype(BF)
    mask1 = dot(flags_t, ones_where(iota((16, 512), 0) == (iota((16, 512), 1) >> 5)).astype(BF), 0, 0)
    mask2 = dot(flags_t, ones_where(iota((16, 512), 0) == (iota((16, 512), 1) & 15)).astype(BF), 0, 0)
    mask1_ref[...] = mask1
    mask2_ref[...] = mask2
    flags_t = jnp.concatenate([flags_t, jnp.zeros((16, 96), BF)], axis=1)
    parts = [proj_ref[pl.ds(i, 32, stride=16), :] for i in range(16)]
    lw = (jnp.concatenate([p[:, 0:32] for p in parts], axis=1) * mask1).astype(BF)
    rw = jnp.concatenate([p[:, 32:64] for p in parts], axis=1).astype(BF)
    rw = (dot(rw, perm1) * mask2).astype(BF)
    for l in range(4):
        for h in range(2):
            lall[zl, y, 2 * l + h] = lw[16 * h : 16 * h + 16, 128 * l : 128 * l + 128]
            wire[2 * l + h] = rw[16 * h : 16 * h + 16, 128 * l : 128 * l + 128]
    lall[zl, y, 8] = flags_t
    wire[8] = flags_t

    pl.semaphore_wait(barrier, 23 + crossed)

    zcopies = {}
    for d in (2, 1, 3, 0):
        zcopies[d] = remote(
            wire, zbuf.at[zh], zs.at[d], zr.at[d], device(x_=tx, zl_=tzl, zh_=rem(zh + d, 4))
        )
    for d in (2, 1, 3):
        zcopies[d].start()

    @pl.when(crossed == 1)
    def _():
        zcopies[0].start()

    @pl.when(crossed == 0)
    def _():
        pltpu.make_async_copy(wire, zbuf.at[zh], zr.at[0]).start()

    lcopies = [
        remote(
            lall.at[zl, y], lall.at[zl, y], ls.at[k - 1], lr.at[k - 1],
            device(y_=rem(y + k // 2, 4), zl_=rem(zl + k % 2, 2)),
        )
        for k in range(1, 8)
    ]

    def send_left():
        for c in lcopies:
            c.start()

    jb = 2 * rem(tx, 2) + core
    bcopies = {}

    def spread_out(d):
        t = rem(zh + 4 - d, 4)
        landed(zbuf.at[t], zr.at[d])
        for dx in (2, 1, 3, 0):
            c = remote(
                zbuf.at[t], rall.at[jb, tzl, y], bs.at[d, dx], br.at[x, y], device(x_=rem(x + dx, 4), y_=t)
            )
            bcopies[d, dx] = c
            if dx:
                c.start()
            else:

                @pl.when(t == y)
                def _():
                    pltpu.make_async_copy(zbuf.at[t], rall.at[jb, tzl, y], br.at[x, y]).start()

                @pl.when(t != y)
                def _():
                    c.start()

    spread_out(0)
    send_left()
    for c in inputs[8:]:
        c.wait()
    wf_ref[...] = wm_ref[...].astype(F32)
    for e in range(32):
        wec_ref[32 * e : 32 * e + 32, :] = wf_ref[pl.ds(e, 32, stride=32), :].astype(BF)
    dt_ref[...] = delta_ref[...].astype(F32).reshape(1024, 128).T.astype(BF)
    spread_out(1)
    spread_out(3)
    perm2_ref[...] = ones_where(
        ((rows >> 7) == ((cols >> 4) & 3)) & (((rows >> 4) & 7) == (cols >> 6)) & ((rows & 15) == (cols & 15))
    ).astype(BF)
    wt_ref[...] = wec_ref[...].astype(F32).T.astype(BF)
    spread_out(2)

    for l in range(4):
        tile_ref[...] = dot(wec_ref[256 * l : 256 * l + 256, :], dt_ref[...])

        def spread_pair(p, carry, l=l):
            lanes = pl.ds(pl.multiple_of(p * 128, 128), 128)
            for t in range(4):
                a, b = swap_halves(tile_ref[64 * t : 64 * t + 32, lanes], tile_ref[64 * t + 32 : 64 * t + 64, lanes])
                place = slice(512 * l + 128 * t, 512 * l + 128 * t + 128)
                d_ref[pl.ds(pl.multiple_of(p * 64, 64), 32), place] = a.astype(BF)
                d_ref[pl.ds(pl.multiple_of(p * 64 + 32, 32), 32), place] = b.astype(BF)
            return carry

        lax.fori_loop(0, 8, spread_pair, 0)

    ccopies = []
    for n, (dx, dy) in enumerate(NEAR):
        xs, ys = rem(x + dx, 4), rem(y + dy, 4)
        gx_, gzl_ = twin(xs)
        block = rall.at[2 * rem(gx_, 2) + core, gzl_, ys]
        landed(block, br.at[xs, ys])
        c = remote(block, block, cs.at[n], cr.at[n], device(core_=other))
        c.start()
        ccopies.append(c)
    for c in lcopies:
        c.wait_recv()
    for b in range(8):
        for l in range(4):
            for h in range(2):
                left_ref[32 * b + 16 * h : 32 * b + 16 * h + 16, 128 * l : 128 * l + 128] = lall[b // 4, b % 4, 2 * l + h]
    for c in ccopies:
        c.wait_recv()

    mi = jnp.concatenate([lall[b // 4, b % 4, 8] for b in range(8)], axis=1)
    mj = jnp.concatenate(
        [jnp.concatenate([rall[g, b // 4, b % 4, 8] for b in range(8)], axis=1) for g in range(4)], axis=0
    )
    count = dot(mi, mj, 1, 1)
    count = dot(count.astype(BF), ones_where(iota((64, 128), 0) == (iota((64, 128), 1) & 63)).astype(BF))
    rec_ref[...] = 1.0 / (count + 0.001)

    def scale(i, carry):
        here = pl.ds(pl.multiple_of(i * 32, 32), 32)
        factor = jnp.broadcast_to(rec_ref[pl.ds(i, 1), :], (32, 128))
        for t in range(16):
            lanes = slice(128 * t, 128 * t + 128)
            d_ref[here, lanes] = (d_ref[here, lanes].astype(F32) * factor).astype(BF)
        return carry

    lax.fori_loop(0, 16, scale, 0)

    gcopies = []
    for n in range(2):
        half = rem(tzl + 1 + n, 2)
        part = dot(left_ref[pl.ds(pl.multiple_of(half * 128, 128), 128), :], d_ref[...]).astype(BF)
        for l in range(4):
            piece = dot(part[:, 512 * l : 512 * l + 512], perm2_ref[...], 1, 1).astype(BF)
            for g in range(4):
                gsend[half, g % 2, g // 2, :, 2 * l : 2 * l + 2] = piece[:, 128 * g : 128 * g + 128].reshape(4, 2, 16, 128)
        c = remote(gsend.at[half, other], gcore.at[half], gcs.at[n], gcr.at[n], device(core_=other))
        c.start()
        gcopies.append(c)

    gbcopies = []
    for n in range(2):
        half = rem(tzl + 1 + n, 2)
        gcopies[n].wait_recv()
        hsend[half] = (gsend[half, core].astype(F32) + gcore[half].astype(F32)).astype(BF)
        for m in range(2):
            x_ = 2 * rem(div(x, 2) + 1 + n, 2) + rem(x + 1 + m, 2)
            hx, _ = twin(x_)
            for dy in (2, 1, 3, 0):
                y_ = rem(y + dy, 4)
                src = hsend.at[half, rem(hx, 2), y_]
                if n == 1 and m == 1 and dy == 0:
                    pltpu.make_async_copy(src, gx.at[x, y], gbr.at[x, y]).start()
                else:
                    c = remote(src, gx.at[x, y], gbs.at[n, m, dy], gbr.at[x, y], device(x_=x_, y_=y_))
                    c.start()
                    gbcopies.append(c)

    for l in range(4):
        packed = jnp.concatenate([rall[g, :, :, 2 * l : 2 * l + 2].reshape(256, 128) for g in range(4)], axis=1)
        right_ref[:, 512 * l : 512 * l + 512] = dot(packed, perm2_ref[...]).astype(BF)
    part = dot(right_ref[...], d_ref[...], 1, 1)
    lsend[...] = part.astype(BF).reshape(8, 32, 512)
    glcopies = []
    for k in (4, 5, 2, 3, 6, 7, 1):
        y_, zl_ = rem(y + k // 2, 4), rem(zl + k % 2, 2)
        c = remote(lsend.at[zl_ * 4 + y_], lrecv.at[k - 1], gls.at[k - 1], glr.at[k - 1], device(y_=y_, zl_=zl_))
        c.start()
        glcopies.append(c)

    def pair_part(l):
        o = dot(left_ref[...], right_ref[:, 512 * l : 512 * l + 512], 0, 0)
        for t in range(4):
            for p in range(8):
                a, b = swap_halves(
                    o[64 * p : 64 * p + 32, 128 * t : 128 * t + 128],
                    o[64 * p + 32 : 64 * p + 64, 128 * t : 128 * t + 128],
                )
                tile_ref[64 * t : 64 * t + 32, 128 * p : 128 * p + 128] = a
                tile_ref[64 * t + 32 : 64 * t + 64, 128 * p : 128 * p + 128] = b
        term = dot(wt_ref[:, 256 * l : 256 * l + 256], tile_ref[...].astype(BF))
        if l == 0:
            pt_ref[...] = term
        else:
            pt_ref[...] += term

    pair_part(0)
    pair_part(1)

    gzcopies = {}
    for d in (2, 1, 3, 0):
        t = rem(zh + d, 4)
        for s in range(4):
            landed(gx.at[s, t], gbr.at[s, t])
        total = gx[0, t].astype(F32) + gx[1, t].astype(F32) + gx[2, t].astype(F32) + gx[3, t].astype(F32)
        ksend[t] = total.astype(BF)
        c = remote(ksend.at[t], gz.at[zh], gzs.at[d], gzr.at[d], device(x_=tx, zl_=tzl, zh_=t))
        gzcopies[d] = c
        if d:
            c.start()
        else:

            @pl.when(crossed == 1)
            def _():
                c.start()

            @pl.when(crossed == 0)
            def _():
                pltpu.make_async_copy(ksend.at[zh], gz.at[zh], gzr.at[0]).start()

    pair_part(2)
    pair_part(3)
    factor = jnp.concatenate(
        [
            jnp.where(iota((1, 128), 1) < 64, rec_ref[2 * p : 2 * p + 1, :], rec_ref[2 * p + 1 : 2 * p + 2, :])
            for p in range(8)
        ],
        axis=1,
    )
    pair_ref[...] = (pt_ref[...] * factor).T.astype(BF).reshape(16, 64, 128)

    for c in glcopies:
        c.wait_recv()
    dl = lsend[zl * 4 + y].astype(F32)
    for k in range(7):
        dl = dl + lrecv[k].astype(F32)
    dl = dl * mask1_ref[...]

    for d in (0, 1, 3, 2):
        t = rem(zh + 4 - d, 4)
        landed(gz.at[t], gzr.at[d])
    total = gz[0].astype(F32) + gz[1].astype(F32) + gz[2].astype(F32) + gz[3].astype(F32)
    dr = jnp.concatenate(
        [jnp.concatenate([total[2 * l], total[2 * l + 1]], axis=0) for l in range(4)], axis=1
    ) * mask2_ref[...]
    hi, lo = split(dr)
    dr = dot(hi, perm1_ref[...], 1, 1) + dot(lo, perm1_ref[...], 1, 1)

    rows_i = jnp.concatenate(
        [
            jnp.concatenate([dl[:, 32 * i : 32 * i + 32], dr[:, 32 * i : 32 * i + 32]], axis=1)
            for i in range(16)
        ],
        axis=0,
    )
    hi, lo = split(rows_i)
    dn = dot(hi, w) + dot(lo, w)
    for i in range(16):
        for h in range(2):
            dn_ref[h, pl.ds(i, 32, stride=16), :] = dn[32 * i : 32 * i + 32, 128 * h : 128 * h + 128]
    dn = jnp.concatenate([dn_ref[0], dn_ref[1]], axis=1) * gain_ref[...]
    xhat = xhat_ref[...]
    dx = rstd_ref[:, 0:1] * (
        dn - jnp.mean(dn, axis=-1, keepdims=True) - xhat * jnp.mean(dn * xhat, axis=-1, keepdims=True)
    )
    grad_ref[...] = dx.astype(BF).reshape(32, 16, 256)

    for c in lcopies + ccopies + gcopies + glcopies + gbcopies:
        c.wait_send()
    for d in (1, 2, 3):
        zcopies[d].wait_send()
        gzcopies[d].wait_send()

    @pl.when(crossed == 1)
    def _():
        zcopies[0].wait_send()
        gzcopies[0].wait_send()

    for d in range(4):
        for dx in (1, 2, 3):
            bcopies[d, dx].wait_send()

        @pl.when(rem(zh + 4 - d, 4) != y)
        def _():
            bcopies[d, 0].wait_send()


def body(
    homolog_stack,
    presence_flags,
    normalizer_scaling,
    normalizer_offset,
    first_factor_matrix,
    first_factor_offset,
    second_factor_matrix,
    second_factor_offset,
    final_mapping_matrix,
    coupling_delta_cotangent,
):
    dma = pltpu.SemaphoreType.DMA
    vm = pltpu.VMEM
    whole = pl.BlockSpec(memory_space=pltpu.VMEM)
    far = pl.BlockSpec(memory_space=pltpu.HBM)
    return tuple(
        pl.pallas_call(
            kernel,
            out_shape=(
                jax.ShapeDtypeStruct((16, 64, 128), BF),
                jax.ShapeDtypeStruct((32, 16, 256), BF),
            ),
            in_specs=[far] * 10,
            out_specs=(whole, whole),
            scratch_shapes=[
                vm((32, 16, 256), BF),
                vm((16, 32), jnp.int32),
                vm((1, 256), F32),
                vm((1, 256), F32),
                vm((32, 256), BF),
                vm((1, 32), F32),
                vm((32, 256), BF),
                vm((1, 32), F32),
                vm((1024, 128), BF),
                vm((16, 64, 128), BF),
                dma((10,)),
                vm((512, 256), F32),
                vm((512, 128), F32),
                vm((512, 128), F32),
                vm((1024, 128), F32),
                vm((1024, 128), BF),
                vm((128, 1024), BF),
                vm((128, 1024), BF),
                vm((32, 512), F32),
                vm((32, 512), F32),
                vm((512, 512), BF),
                vm((512, 512), BF),
                vm((9, 16, 128), BF),
                vm((4, 9, 16, 128), BF),
                vm((2, 4, 9, 16, 128), BF),
                vm((4, 2, 4, 9, 16, 128), BF),
                vm((256, 512), BF),
                vm((256, 2048), BF),
                vm((256, 1024), F32),
                vm((512, 2048), BF),
                vm((16, 128), F32),
                vm((128, 1024), F32),
                vm((2, 2, 2, 4, 8, 16, 128), BF),
                vm((2, 2, 4, 8, 16, 128), BF),
                vm((2, 2, 4, 8, 16, 128), BF),
                vm((4, 4, 8, 16, 128), BF),
                vm((4, 8, 16, 128), BF),
                vm((4, 8, 16, 128), BF),
                vm((8, 32, 512), BF),
                vm((7, 32, 512), BF),
                vm((2, 512, 128), F32),
                dma((4,)), dma((4,)),
                dma((4, 4)), dma((4, 4)),
                dma((16,)), dma((16,)),
                dma((7,)), dma((7,)),
                dma((2,)), dma((2,)),
                dma((2, 2, 4)), dma((4, 4)),
                dma((4,)), dma((4,)),
                dma((7,)), dma((7,)),
            ],
            compiler_params=pltpu.CompilerParams(
                collective_id=0, has_side_effects=True, vmem_limit_bytes=63 * 1024 * 1024
            ),
        )(
            homolog_stack,
            presence_flags.T,
            normalizer_scaling.reshape(1, 256),
            normalizer_offset.reshape(1, 256),
            first_factor_matrix.T,
            first_factor_offset.reshape(1, 32),
            second_factor_matrix.T,
            second_factor_offset.reshape(1, 32),
            final_mapping_matrix,
            coupling_delta_cotangent,
        )
    )


def solution(mesh):
    return jax.shard_map(
        body,
        mesh=mesh,
        in_specs=(
            P("seq", "res", None),
            P("seq", "res"),
            P(),
            P(),
            P(),
            P(),
            P(),
            P(),
            P(),
            P("res", "seq", None),
        ),
        out_specs=(P("res", "seq", None), P("seq", "res", None)),
        check_vma=False,
    )
```

```python
import jax
import jax.numpy as jnp
from jax import lax
from jax.experimental import pallas as pl
from jax.experimental.pallas import tpu as pltpu
from jax.sharding import PartitionSpec as P

F32 = jnp.float32
BF = jnp.bfloat16
MESH = pl.DeviceIdType.MESH


def dot(a, b, ca=1, cb=0):
    return lax.dot_general(a, b, (((ca,), (cb,)), ((), ())), preferred_element_type=F32)


def rem(a, n):
    return lax.rem(a, jnp.int32(n))


def div(a, n):
    return lax.div(a, jnp.int32(n))


def split(a):
    hi = a.astype(BF)
    return hi, (a - hi.astype(F32)).astype(BF)


def ones_where(condition):
    return jnp.where(condition, 1.0, 0.0)


def iota(shape, dim):
    return lax.broadcasted_iota(jnp.int32, shape, dim)


def swap_halves(a, b):
    low = iota(a.shape, 1) < 64
    return (
        jnp.where(low, a, pltpu.roll(b, 64, 1)),
        jnp.where(low, pltpu.roll(a, 64, 1), b),
    )


NEAR = ((0, 0), (0, 1), (0, 3), (1, 0), (3, 0), (1, 1), (1, 3), (3, 1), (3, 3), (0, 2), (2, 0), (1, 2), (3, 2), (2, 1), (2, 3), (2, 2))


def kernel(
    x_hbm, flag_hbm, gain_hbm, shift_hbm, w1_hbm, b1_hbm, w2_hbm, b2_hbm, wm_hbm, delta_hbm,
    pair_ref, grad_ref,
    x_ref, flag_ref, gain_ref, shift_ref, w1_ref, b1_ref, w2_ref, b2_ref, wm_ref, delta_ref, in_sem,
    xhat_ref, rstd_ref, proj_ref, wf_ref, wec_ref, wt_ref, dt_ref, mask1_ref, mask2_ref, perm1_ref, perm2_ref,
    fwire, fz, fall, wire, zbuf, lall, rall, left_ref, right_ref, tile_ref, draw_ref, d_ref, rec_ref, pt_ref,
    own_ref, gsend, gcore, hsend, gx, ksend, gz, lsend, lrecv, lsum, lother, dnl_ref, dn_ref,
    fzs, fzr, fbs, fbr, fcs, fcr, zs, zr, bs, br, cs, cr, ls, lr,
    gcs, gcr, gbs, gbr, gzs, gzr, gls, glr,
):
    inputs = [
        pltpu.make_async_copy(a, b, in_sem.at[n])
        for n, (a, b) in enumerate(
            zip(
                (x_hbm, flag_hbm, gain_hbm, shift_hbm, w1_hbm, b1_hbm, w2_hbm, b2_hbm, wm_hbm, delta_hbm),
                (x_ref, flag_ref, gain_ref, shift_ref, w1_ref, b1_ref, w2_ref, b2_ref, wm_ref, delta_ref),
            )
        )
    ]
    for c in inputs:
        c.start()

    q = lax.axis_index("seq")
    r = lax.axis_index("res")
    y, zl = div(q, 2), rem(q, 2)
    zh, x, core = div(r, 8), rem(div(r, 2), 4), rem(r, 2)
    other = 1 - core

    def device(x_=x, y_=y, zh_=zh, zl_=zl, core_=core):
        return {"seq": y_ * 2 + zl_, "res": zh_ * 8 + x_ * 2 + core_}

    def twin(x_):
        m = rem(div(x_, 2) + zl, 2)
        return x_ + m * (3 - 2 * x_), rem(zl + m, 2)

    crossed = rem(div(x, 2) + zl, 2)
    tx, tzl = twin(x)

    def remote(src, dst, send, recv, where):
        return pltpu.make_async_remote_copy(
            src_ref=src, dst_ref=dst, send_sem=send, recv_sem=recv, device_id=where, device_id_type=MESH
        )

    def landed(ref, sem):
        pltpu.make_async_copy(ref, ref, sem).wait()

    barrier = pltpu.get_barrier_semaphore()

    def greet(where):
        pl.semaphore_signal(barrier, inc=1, device_id=where, device_id_type=MESH)

    for d in (2, 1, 3):
        greet(device(x_=tx, zl_=tzl, zh_=rem(zh + d, 4)))

    @pl.when(crossed == 1)
    def _():
        greet(device(x_=tx, zl_=tzl))

    for dx, dy in NEAR[1:]:
        greet(device(x_=rem(x + dx, 4), y_=rem(y + dy, 4)))
    for dy in range(4):
        greet(device(y_=rem(y + dy, 4), zl_=1 - zl))
    greet(device(core_=other))

    inputs[1].wait()
    flags_t = flag_ref[...].astype(F32).astype(BF)
    flags_tile = jnp.concatenate([flags_t, jnp.zeros((16, 96), BF)], axis=1)
    fwire[...] = flags_tile
    lall[zl, y, 8] = flags_tile

    def over_z(src, buf, send, recv):
        copies = {}
        for d in (2, 1, 3, 0):
            copies[d] = remote(src, buf.at[zh], send.at[d], recv.at[d], device(x_=tx, zl_=tzl, zh_=rem(zh + d, 4)))
        for d in (2, 1, 3):
            copies[d].start()

        @pl.when(crossed == 1)
        def _():
            copies[0].start()

        @pl.when(crossed == 0)
        def _():
            pltpu.make_async_copy(src, buf.at[zh], recv.at[0]).start()

        return copies

    def spread_out(d, buf, zrecv, dst, send, recv):
        t = rem(zh + 4 - d, 4)
        landed(buf.at[t], zrecv.at[d])
        place = dst.at[core, rem(tx, 2), tzl, y]
        copies = []
        for dx in (2, 1, 3, 0):
            c = remote(buf.at[t], place, send.at[d, dx], recv.at[x, y], device(x_=rem(x + dx, 4), y_=t))
            copies.append(c)
            if dx:
                c.start()
            else:

                @pl.when(t == y)
                def _():
                    pltpu.make_async_copy(buf.at[t], place, recv.at[x, y]).start()

                @pl.when(t != y)
                def _():
                    c.start()

        return copies

    rows, cols = iota((512, 512), 0), iota((512, 512), 1)
    perm1 = ones_where(((rows >> 5) == (cols & 15)) & ((rows & 31) == (cols >> 4))).astype(BF)
    perm1_ref[...] = perm1
    for n in (0, 2, 3, 4, 5, 6, 7):
        inputs[n].wait()
    xv = x_ref[...].astype(F32).reshape(512, 256)
    centred = xv - jnp.mean(xv, axis=-1, keepdims=True)
    rstd = lax.rsqrt(jnp.mean(centred * centred, axis=-1, keepdims=True) + 1e-5)
    xhat = centred * rstd
    xhat_ref[...] = xhat
    rstd_ref[...] = jnp.broadcast_to(rstd, (512, 128))
    hi, lo = split(xhat * gain_ref[...] + shift_ref[...])
    w = jnp.concatenate([w1_ref[...], w2_ref[...]], axis=0)
    bias = jnp.concatenate([b1_ref[...], b2_ref[...]], axis=1)
    proj_ref[:, 0:64] = dot(hi, w, 1, 1) + dot(lo, w, 1, 1) + bias

    mask1 = dot(flags_t, ones_where(iota((16, 512), 0) == (iota((16, 512), 1) >> 5)).astype(BF), 0, 0)
    mask2 = dot(flags_t, ones_where(iota((16, 512), 0) == (iota((16, 512), 1) & 15)).astype(BF), 0, 0)
    mask1_ref[...] = mask1
    mask2_ref[...] = mask2
    parts = [proj_ref[pl.ds(i, 32, stride=16), :] for i in range(16)]
    lw = (jnp.concatenate([p[:, 0:32] for p in parts], axis=1) * mask1).astype(BF)
    rw = jnp.concatenate([p[:, 32:64] for p in parts], axis=1).astype(BF)
    rw = (dot(rw, perm1) * mask2).astype(BF)
    for l in range(4):
        for h in range(2):
            lall[zl, y, 2 * l + h] = lw[16 * h : 16 * h + 16, 128 * l : 128 * l + 128]
            wire[2 * l + h] = rw[16 * h : 16 * h + 16, 128 * l : 128 * l + 128]
    pl.semaphore_wait(barrier, 23 + crossed)
    fzcopies = over_z(fwire, fz, fzs, fzr)
    zcopies = over_z(wire, zbuf, zs, zr)
    lcopies = [
        remote(
            lall.at[zl, y], lall.at[zl, y], ls.at[k - 1], lr.at[k - 1],
            device(y_=rem(y + k // 2, 4), zl_=rem(zl + k % 2, 2)),
        )
        for k in range(1, 8)
    ]

    for c in lcopies:
        c.start()

    fbcopies, bcopies = {}, {}

    def spread_flags(d):
        fbcopies[d] = spread_out(d, fz, fzr, fall, fbs, fbr)

    def spread_right(d):
        bcopies[d] = spread_out(d, zbuf, zr, rall, bs, br)

    spread_flags(0)
    spread_right(0)
    for c in inputs[8:]:
        c.wait()
    wf_ref[...] = wm_ref[...].astype(F32)
    for e in range(32):
        wec_ref[32 * e : 32 * e + 32, :] = wf_ref[pl.ds(e, 32, stride=32), :].astype(BF)
    dt_ref[...] = delta_ref[...].astype(F32).reshape(1024, 128).T.astype(BF)
    perm2_ref[...] = ones_where(
        ((rows >> 7) == ((cols >> 4) & 3)) & (((rows >> 4) & 7) == (cols >> 6)) & ((rows & 15) == (cols & 15))
    ).astype(BF)
    spread_flags(1)
    spread_flags(3)
    spread_right(1)
    spread_right(3)

    def product(l):
        tile_ref[...] = dot(wec_ref[256 * l : 256 * l + 256, :], dt_ref[...])

        def spread_pair(p, carry):
            lanes = pl.ds(pl.multiple_of(p * 128, 128), 128)
            for t in range(4):
                a, b = swap_halves(tile_ref[64 * t : 64 * t + 32, lanes], tile_ref[64 * t + 32 : 64 * t + 64, lanes])
                place = slice(128 * t, 128 * t + 128)
                draw_ref[pl.ds(pl.multiple_of(p * 64, 64), 32), place] = a.astype(BF)
                draw_ref[pl.ds(pl.multiple_of(p * 64 + 32, 32), 32), place] = b.astype(BF)
            return carry

        lax.fori_loop(0, 8, spread_pair, 0)
        part = dot(draw_ref[...], perm2_ref[...], 1, 1).astype(BF)
        for g in range(4):
            place = slice(256 * l + 128 * (g // 2), 256 * l + 128 * (g // 2) + 128)
            d_ref[g % 2, :, place] = part[:, 128 * g : 128 * g + 128]

    spread_flags(2)
    product(0)
    product(1)
    product(2)
    spread_right(2)
    product(3)

    for xs in range(4):
        for ys in range(4):
            landed(fall.at[0, 0, 0, 0], fbr.at[xs, ys])
    fcopy = remote(fall.at[core], fall.at[core], fcs.at[0], fcr.at[0], device(core_=other))
    fcopy.start()
    for c in lcopies:
        c.wait_recv()
    for b in range(8):
        for l in range(4):
            for h in range(2):
                left_ref[32 * b + 16 * h : 32 * b + 16 * h + 16, 128 * l : 128 * l + 128] = lall[b // 4, b % 4, 2 * l + h]
    fcopy.wait_recv()

    mi = jnp.concatenate([lall[b // 4, b % 4, 8] for b in range(8)], axis=1)
    mj = jnp.concatenate(
        [jnp.concatenate([fall[g % 2, g // 2, b // 4, b % 4] for b in range(8)], axis=1) for g in range(4)], axis=0
    )
    count = dot(mi, mj, 1, 1).astype(BF)
    lane = iota((64, 512), 1)
    spread = dot(count, ones_where(iota((64, 512), 0) == ((lane >> 7) * 16 + (lane & 15))).astype(BF))
    spread = 1.0 / (spread + 0.001)
    for g in range(4):
        rec_ref[g] = spread[:, 128 * g : 128 * g + 128]

    def scale(i, carry):
        here = pl.ds(pl.multiple_of(i * 32, 32), 32)
        for g in range(4):
            factor = jnp.broadcast_to(rec_ref[g, pl.ds(i, 1), :], (32, 128))
            for l in range(4):
                lanes = slice(256 * l + 128 * (g // 2), 256 * l + 128 * (g // 2) + 128)
                d_ref[g % 2, here, lanes] = (d_ref[g % 2, here, lanes].astype(F32) * factor).astype(BF)
        return carry

    lax.fori_loop(0, 16, scale, 0)

    part = dot(left_ref[...], d_ref[other]).astype(BF)
    for l in range(4):
        for g in range(2):
            lanes = slice(256 * l + 128 * g, 256 * l + 128 * g + 128)
            gsend[:, g, :, 2 * l : 2 * l + 2] = part[:, lanes].reshape(2, 4, 2, 16, 128)
    gcopies = []
    for n in range(2):
        half = rem(tzl + 1 + n, 2)
        c = remote(gsend.at[half], gcore.at[half], gcs.at[n], gcr.at[n], device(core_=other))
        c.start()
        gcopies.append(c)
    part = dot(left_ref[...], d_ref[core])
    for l in range(4):
        for g in range(2):
            lanes = slice(256 * l + 128 * g, 256 * l + 128 * g + 128)
            own_ref[:, g, :, 2 * l : 2 * l + 2] = part[:, lanes].reshape(2, 4, 2, 16, 128)

    gbcopies = []
    for n in range(2):
        half = rem(tzl + 1 + n, 2)
        gcopies[n].wait_recv()
        hsend[half] = (own_ref[half] + gcore[half].astype(F32)).astype(BF)
        for m in range(2):
            x_ = 2 * rem(div(x, 2) + 1 + n, 2) + rem(x + 1 + m, 2)
            hx, _ = twin(x_)
            for dy in (2, 1, 3, 0):
                y_ = rem(y + dy, 4)
                src = hsend.at[half, rem(hx, 2), y_]
                if n == 1 and m == 1 and dy == 0:
                    pltpu.make_async_copy(src, gx.at[x, y], gbr.at[x, y]).start()
                else:
                    c = remote(src, gx.at[x, y], gbs.at[n, m, dy], gbr.at[x, y], device(x_=x_, y_=y_))
                    c.start()
                    gbcopies.append(c)

    ccopies = []
    for n, (dx, dy) in enumerate(NEAR):
        xs, ys = rem(x + dx, 4), rem(y + dy, 4)
        gx_, gzl_ = twin(xs)
        block = rall.at[core, rem(gx_, 2), gzl_, ys]
        landed(block, br.at[xs, ys])
        c = remote(block, block, cs.at[n], cr.at[n], device(core_=other))
        c.start()
        ccopies.append(c)
    for c in ccopies:
        c.wait_recv()

    part = 0.0
    for g in range(2):
        for l in range(4):
            packed = jnp.concatenate(
                [rall[g, h, :, :, 2 * l : 2 * l + 2].reshape(256, 128) for h in range(2)], axis=1
            )
            part = part + dot(packed, d_ref[g, :, 256 * l : 256 * l + 256], 1, 1)
    part = part.astype(BF)
    for b in range(8):
        lsend[b % 4, b // 4] = part[32 * b : 32 * b + 32]
    glcopies = []
    for dy in (2, 1, 3):
        y_ = rem(y + dy, 4)
        c = remote(lsend.at[y_], lrecv.at[dy - 1], gls.at[dy], glr.at[dy], device(y_=y_))
        c.start()
        glcopies.append(c)

    def pair_part(l):
        packed = jnp.concatenate(
            [rall[g % 2, g // 2, :, :, 2 * l : 2 * l + 2].reshape(256, 128) for g in range(4)], axis=1
        )
        right_ref[...] = dot(packed, perm2_ref[...]).astype(BF)
        o = dot(left_ref[...], right_ref[...], 0, 0)
        for t in range(4):
            for p in range(8):
                a, b = swap_halves(
                    o[64 * p : 64 * p + 32, 128 * t : 128 * t + 128],
                    o[64 * p + 32 : 64 * p + 64, 128 * t : 128 * t + 128],
                )
                tile_ref[64 * t : 64 * t + 32, 128 * p : 128 * p + 128] = a
                tile_ref[64 * t + 32 : 64 * t + 64, 128 * p : 128 * p + 128] = b
        term = dot(wt_ref[:, 256 * l : 256 * l + 256], tile_ref[...].astype(BF))
        if l == 0:
            pt_ref[...] = term
        else:
            pt_ref[...] += term

    wt_ref[...] = wec_ref[...].astype(F32).T.astype(BF)
    pair_part(0)

    gzcopies = {}
    for d in (2, 1, 3, 0):
        t = rem(zh + d, 4)
        for s in range(4):
            landed(gx.at[s, t], gbr.at[s, t])
        total = gx[0, t].astype(F32) + gx[1, t].astype(F32) + gx[2, t].astype(F32) + gx[3, t].astype(F32)
        ksend[t] = total.astype(BF)
        c = remote(ksend.at[t], gz.at[zh], gzs.at[d], gzr.at[d], device(x_=tx, zl_=tzl, zh_=t))
        gzcopies[d] = c
        if d:
            c.start()
        else:

            @pl.when(crossed == 1)
            def _():
                c.start()

            @pl.when(crossed == 0)
            def _():
                pltpu.make_async_copy(ksend.at[zh], gz.at[zh], gzr.at[0]).start()

    for c in glcopies:
        c.wait_recv()
    dl = lsend[y].astype(F32) + lrecv[0].astype(F32) + lrecv[1].astype(F32) + lrecv[2].astype(F32)
    lsum[...] = dl.astype(BF)
    glcross = remote(lsum.at[1 - zl], lother, gls.at[0], glr.at[0], device(zl_=1 - zl))
    glcross.start()
    glcopies.append(glcross)
    pair_part(1)
    pair_part(2)
    pair_part(3)
    count = dot(count, ones_where(iota((64, 128), 0) == (iota((64, 128), 1) & 63)).astype(BF)) + 0.001
    low = iota((1, 128), 1) < 64
    denom = jnp.concatenate(
        [jnp.where(low, count[2 * p : 2 * p + 1], count[2 * p + 1 : 2 * p + 2]) for p in range(8)], axis=1
    )
    pair_ref[...] = (pt_ref[...] / denom).T.astype(BF).reshape(16, 64, 128)

    glcross.wait_recv()
    dl = (lsum[zl].astype(F32) + lother[...].astype(F32)) * mask1_ref[...]
    hi, lo = split(jnp.concatenate([dl[:, 32 * i : 32 * i + 32] for i in range(16)], axis=0))
    dnl_ref[...] = dot(hi, w1_ref[...]) + dot(lo, w1_ref[...])

    for d in (0, 1, 3, 2):
        t = rem(zh + 4 - d, 4)
        landed(gz.at[t], gzr.at[d])
    total = gz[0].astype(F32) + gz[1].astype(F32) + gz[2].astype(F32) + gz[3].astype(F32)
    dr = jnp.concatenate(
        [jnp.concatenate([total[2 * l], total[2 * l + 1]], axis=0) for l in range(4)], axis=1
    ) * mask2_ref[...]
    hi, lo = split(dr)
    dr = dot(hi, perm1_ref[...], 1, 1) + dot(lo, perm1_ref[...], 1, 1)

    hi, lo = split(jnp.concatenate([dr[:, 32 * i : 32 * i + 32] for i in range(16)], axis=0))
    dn = dnl_ref[...] + dot(hi, w2_ref[...]) + dot(lo, w2_ref[...])
    for i in range(16):
        for h in range(2):
            dn_ref[h, pl.ds(i, 32, stride=16), :] = dn[32 * i : 32 * i + 32, 128 * h : 128 * h + 128]
    dn = jnp.concatenate([dn_ref[0], dn_ref[1]], axis=1) * gain_ref[...]
    xhat = xhat_ref[...]
    dx = rstd_ref[:, 0:1] * (
        dn - jnp.mean(dn, axis=-1, keepdims=True) - xhat * jnp.mean(dn * xhat, axis=-1, keepdims=True)
    )
    grad_ref[...] = dx.astype(BF).reshape(32, 16, 256)

    for c in [fcopy] + lcopies + ccopies + gcopies + glcopies + gbcopies:
        c.wait_send()
    for d in (1, 2, 3):
        fzcopies[d].wait_send()
        zcopies[d].wait_send()
        gzcopies[d].wait_send()

    @pl.when(crossed == 1)
    def _():
        fzcopies[0].wait_send()
        zcopies[0].wait_send()
        gzcopies[0].wait_send()

    for d in range(4):
        for c in fbcopies[d][:3] + bcopies[d][:3]:
            c.wait_send()

        @pl.when(rem(zh + 4 - d, 4) != y)
        def _():
            fbcopies[d][3].wait_send()
            bcopies[d][3].wait_send()


def body(
    homolog_stack,
    presence_flags,
    normalizer_scaling,
    normalizer_offset,
    first_factor_matrix,
    first_factor_offset,
    second_factor_matrix,
    second_factor_offset,
    final_mapping_matrix,
    coupling_delta_cotangent,
):
    dma = pltpu.SemaphoreType.DMA
    vm = pltpu.VMEM
    whole = pl.BlockSpec(memory_space=pltpu.VMEM)
    far = pl.BlockSpec(memory_space=pltpu.HBM)
    return tuple(
        pl.pallas_call(
            kernel,
            out_shape=(
                vm((16, 64, 128), BF),
                vm((32, 16, 256), BF),
            ),
            in_specs=[far] * 10,
            out_specs=(whole, whole),
            scratch_shapes=[
                vm((32, 16, 256), BF),
                vm((16, 32), jnp.int32),
                vm((1, 256), F32),
                vm((1, 256), F32),
                vm((32, 256), BF),
                vm((1, 32), F32),
                vm((32, 256), BF),
                vm((1, 32), F32),
                vm((1024, 128), BF),
                vm((16, 64, 128), BF),
                dma((10,)),
                vm((512, 256), F32),
                vm((512, 128), F32),
                vm((512, 128), F32),
                vm((1024, 128), F32),
                vm((1024, 128), BF),
                vm((128, 1024), BF),
                vm((128, 1024), BF),
                vm((32, 512), F32),
                vm((32, 512), F32),
                vm((512, 512), BF),
                vm((512, 512), BF),
                vm((16, 128), BF),
                vm((4, 16, 128), BF),
                vm((2, 2, 2, 4, 16, 128), BF),
                vm((8, 16, 128), BF),
                vm((4, 8, 16, 128), BF),
                vm((2, 4, 9, 16, 128), BF),
                vm((2, 2, 2, 4, 8, 16, 128), BF),
                vm((256, 512), BF),
                vm((256, 512), BF),
                vm((256, 1024), F32),
                vm((512, 512), BF),
                vm((2, 512, 1024), BF),
                vm((4, 16, 128), F32),
                vm((128, 1024), F32),
                vm((2, 2, 4, 8, 16, 128), F32),
                vm((2, 2, 4, 8, 16, 128), BF),
                vm((2, 2, 4, 8, 16, 128), BF),
                vm((2, 2, 4, 8, 16, 128), BF),
                vm((4, 4, 8, 16, 128), BF),
                vm((4, 8, 16, 128), BF),
                vm((4, 8, 16, 128), BF),
                vm((4, 2, 32, 512), BF),
                vm((3, 2, 32, 512), BF),
                vm((2, 32, 512), BF),
                vm((32, 512), BF),
                vm((512, 256), F32),
                vm((2, 512, 128), F32),
                dma((4,)), dma((4,)),
                dma((4, 4)), dma((4, 4)),
                dma((1,)), dma((1,)),
                dma((4,)), dma((4,)),
                dma((4, 4)), dma((4, 4)),
                dma((16,)), dma((16,)),
                dma((7,)), dma((7,)),
                dma((2,)), dma((2,)),
                dma((2, 2, 4)), dma((4, 4)),
                dma((4,)), dma((4,)),
                dma((4,)), dma((4,)),
            ],
            compiler_params=pltpu.CompilerParams(
                collective_id=0, has_side_effects=True, vmem_limit_bytes=48 * 1024 * 1024
            ),
        )(
            *(
                pltpu.with_memory_space_constraint(a, pltpu.HBM)
                for a in (
                    homolog_stack,
                    presence_flags.T,
                    normalizer_scaling.reshape(1, 256),
                    normalizer_offset.reshape(1, 256),
                    first_factor_matrix.T,
                    first_factor_offset.reshape(1, 32),
                    second_factor_matrix.T,
                    second_factor_offset.reshape(1, 32),
                    final_mapping_matrix,
                    coupling_delta_cotangent,
                )
            )
        )
    )


def solution(mesh):
    return jax.shard_map(
        body,
        mesh=mesh,
        in_specs=(
            P("seq", "res", None),
            P("seq", "res"),
            P(),
            P(),
            P(),
            P(),
            P(),
            P(),
            P(),
            P("res", "seq", None),
        ),
        out_specs=(P("res", "seq", None), P("seq", "res", None)),
        check_vma=False,
    )
```

```python
import jax
import jax.numpy as jnp
from jax import lax
from jax.experimental import pallas as pl
from jax.experimental.pallas import tpu as pltpu
from jax.sharding import PartitionSpec as P

F32 = jnp.float32
BF = jnp.bfloat16
MESH = pl.DeviceIdType.MESH


def dot(a, b, ca=1, cb=0):
    return lax.dot_general(a, b, (((ca,), (cb,)), ((), ())), preferred_element_type=F32)


def rem(a, n):
    return lax.rem(a, jnp.int32(n))


def div(a, n):
    return lax.div(a, jnp.int32(n))


def split(a):
    hi = a.astype(BF)
    return hi, (a - hi.astype(F32)).astype(BF)


def ones_where(condition):
    return jnp.where(condition, 1.0, 0.0)


def iota(shape, dim):
    return lax.broadcasted_iota(jnp.int32, shape, dim)


def swap_halves(a, b):
    low = iota(a.shape, 1) < 64
    return (
        jnp.where(low, a, pltpu.roll(b, 64, 1)),
        jnp.where(low, pltpu.roll(a, 64, 1), b),
    )


NEAR = ((0, 0), (0, 1), (0, 3), (1, 0), (3, 0), (1, 1), (1, 3), (3, 1), (3, 3), (0, 2), (2, 0), (1, 2), (3, 2), (2, 1), (2, 3), (2, 2))


def kernel(
    x_hbm, flag_hbm, gain_hbm, shift_hbm, w1_hbm, b1_hbm, w2_hbm, b2_hbm, wm_hbm, delta_hbm,
    pair_ref, grad_ref,
    x_ref, flag_ref, gain_ref, shift_ref, w1_ref, b1_ref, w2_ref, b2_ref, wm_ref, delta_ref, in_sem,
    xhat_ref, rstd_ref, proj_ref, wf_ref, wec_ref, wt_ref, dt_ref, mask1_ref, mask2_ref, perm1_ref, perm2_ref,
    fwire, fz, fall, wire, zbuf, lall, rall, left_ref, right_ref, tile_ref, draw_ref, d_ref, rec_ref, pt_ref,
    own_ref, gsend, gcore, hsend, gx, ksend, gz, lsend, lrecv, lsum, lother, dnl_ref, dn_ref,
    fzs, fzr, fbs, fbr, fcs, fcr, zs, zr, bs, br, cs, cr, ls, lr,
    gcs, gcr, gbs, gbr, gzs, gzr, gls, glr,
):
    q = lax.axis_index("seq")
    r = lax.axis_index("res")
    y, zl = div(q, 2), rem(q, 2)
    zh, x, core = div(r, 8), rem(div(r, 2), 4), rem(r, 2)
    other = 1 - core

    def device(x_=x, y_=y, zh_=zh, zl_=zl, core_=core):
        return {"seq": y_ * 2 + zl_, "res": zh_ * 8 + x_ * 2 + core_}

    def twin(x_):
        m = rem(div(x_, 2) + zl, 2)
        return x_ + m * (3 - 2 * x_), rem(zl + m, 2)

    crossed = rem(div(x, 2) + zl, 2)
    tx, tzl = twin(x)

    def remote(src, dst, send, recv, where):
        return pltpu.make_async_remote_copy(
            src_ref=src, dst_ref=dst, send_sem=send, recv_sem=recv, device_id=where, device_id_type=MESH
        )

    def landed(ref, sem):
        pltpu.make_async_copy(ref, ref, sem).wait()

    barrier = pltpu.get_barrier_semaphore()

    def greet(where):
        pl.semaphore_signal(barrier, inc=1, device_id=where, device_id_type=MESH)

    for d in (2, 1, 3):
        greet(device(x_=tx, zl_=tzl, zh_=rem(zh + d, 4)))

    @pl.when(crossed == 1)
    def _():
        greet(device(x_=tx, zl_=tzl))

    for dx, dy in NEAR[:0:-1]:
        greet(device(x_=rem(x + dx, 4), y_=rem(y + dy, 4)))
    for dy in range(4):
        greet(device(y_=rem(y + dy, 4), zl_=1 - zl))
    greet(device(core_=other))

    inputs = [
        pltpu.make_async_copy(a, b, in_sem.at[n])
        for n, (a, b) in enumerate(
            zip(
                (x_hbm, flag_hbm, gain_hbm, shift_hbm, w1_hbm, b1_hbm, w2_hbm, b2_hbm, wm_hbm, delta_hbm),
                (x_ref, flag_ref, gain_ref, shift_ref, w1_ref, b1_ref, w2_ref, b2_ref, wm_ref, delta_ref),
            )
        )
    ]
    for c in inputs:
        c.start()

    inputs[1].wait()
    flags_t = flag_ref[...].astype(F32).astype(BF)
    flags_tile = jnp.concatenate([flags_t, jnp.zeros((16, 96), BF)], axis=1)
    fwire[...] = flags_tile
    lall[zl, y, 8] = flags_tile

    def over_z(src, buf, send, recv):
        copies = {}
        for d in (2, 1, 3, 0):
            copies[d] = remote(src, buf.at[zh], send.at[d], recv.at[d], device(x_=tx, zl_=tzl, zh_=rem(zh + d, 4)))
        for d in (2, 1, 3):
            copies[d].start()

        @pl.when(crossed == 1)
        def _():
            copies[0].start()

        @pl.when(crossed == 0)
        def _():
            pltpu.make_async_copy(src, buf.at[zh], recv.at[0]).start()

        return copies

    def spread_out(d, buf, zrecv, dst, send, recv):
        t = rem(zh + 4 - d, 4)
        landed(buf.at[t], zrecv.at[d])
        place = dst.at[core, rem(tx, 2), tzl, y]
        copies = []
        for dx in (2, 1, 3, 0):
            c = remote(buf.at[t], place, send.at[d, dx], recv.at[x, y], device(x_=rem(x + dx, 4), y_=t))
            copies.append(c)
            if dx:
                c.start()
            else:

                @pl.when(t == y)
                def _():
                    pltpu.make_async_copy(buf.at[t], place, recv.at[x, y]).start()

                @pl.when(t != y)
                def _():
                    c.start()

        return copies

    rows, cols = iota((512, 512), 0), iota((512, 512), 1)
    perm1 = ones_where(((rows >> 5) == (cols & 15)) & ((rows & 31) == (cols >> 4))).astype(BF)
    perm1_ref[...] = perm1
    for n in (0, 2, 3, 4, 5, 6, 7):
        inputs[n].wait()
    xv = x_ref[...].astype(F32).reshape(512, 256)
    centred = xv - jnp.mean(xv, axis=-1, keepdims=True)
    rstd = lax.rsqrt(jnp.mean(centred * centred, axis=-1, keepdims=True) + 1e-5)
    xhat = centred * rstd
    xhat_ref[...] = xhat
    rstd_ref[...] = jnp.broadcast_to(rstd, (512, 128))
    hi, lo = split(xhat * gain_ref[...] + shift_ref[...])
    w = jnp.concatenate([w1_ref[...], w2_ref[...]], axis=0)
    bias = jnp.concatenate([b1_ref[...], b2_ref[...]], axis=1)
    proj_ref[:, 0:64] = dot(hi, w, 1, 1) + dot(lo, w, 1, 1) + bias

    mask1 = dot(flags_t, ones_where(iota((16, 512), 0) == (iota((16, 512), 1) >> 5)).astype(BF), 0, 0)
    mask2 = dot(flags_t, ones_where(iota((16, 512), 0) == (iota((16, 512), 1) & 15)).astype(BF), 0, 0)
    mask1_ref[...] = mask1
    mask2_ref[...] = mask2
    parts = [proj_ref[pl.ds(i, 32, stride=16), :] for i in range(16)]
    lw = (jnp.concatenate([p[:, 0:32] for p in parts], axis=1) * mask1).astype(BF)
    rw = jnp.concatenate([p[:, 32:64] for p in parts], axis=1).astype(BF)
    rw = (dot(rw, perm1) * mask2).astype(BF)
    for l in range(4):
        for h in range(2):
            lall[zl, y, 2 * l + h] = lw[16 * h : 16 * h + 16, 128 * l : 128 * l + 128]
            wire[2 * l + h] = rw[16 * h : 16 * h + 16, 128 * l : 128 * l + 128]
    pl.semaphore_wait(barrier, 23 + crossed)
    fzcopies = over_z(fwire, fz, fzs, fzr)
    zcopies = over_z(wire, zbuf, zs, zr)
    lcopies = [
        remote(
            lall.at[zl, y], lall.at[zl, y], ls.at[k - 1], lr.at[k - 1],
            device(y_=rem(y + k // 2, 4), zl_=rem(zl + k % 2, 2)),
        )
        for k in (5, 4, 3, 7, 2, 6, 1)
    ]

    for c in lcopies:
        c.start()

    fbcopies, bcopies = {}, {}

    def spread_flags(d):
        fbcopies[d] = spread_out(d, fz, fzr, fall, fbs, fbr)

    def spread_right(d):
        bcopies[d] = spread_out(d, zbuf, zr, rall, bs, br)

    spread_flags(0)
    spread_right(0)
    spread_flags(1)
    spread_flags(3)
    spread_flags(2)
    spread_right(1)
    spread_right(3)

    def product(l):
        tile_ref[...] = dot(wec_ref[256 * l : 256 * l + 256, :], dt_ref[...])

        def spread_pair(p, carry):
            lanes = pl.ds(pl.multiple_of(p * 128, 128), 128)
            for t in range(4):
                a, b = swap_halves(tile_ref[64 * t : 64 * t + 32, lanes], tile_ref[64 * t + 32 : 64 * t + 64, lanes])
                place = slice(128 * t, 128 * t + 128)
                draw_ref[pl.ds(pl.multiple_of(p * 64, 64), 32), place] = a.astype(BF)
                draw_ref[pl.ds(pl.multiple_of(p * 64 + 32, 32), 32), place] = b.astype(BF)
            return carry

        lax.fori_loop(0, 8, spread_pair, 0)
        part = dot(draw_ref[...], perm2_ref[...], 1, 1).astype(BF)
        for g in range(4):
            place = slice(256 * l + 128 * (g // 2), 256 * l + 128 * (g // 2) + 128)
            d_ref[g % 2, :, place] = part[:, 128 * g : 128 * g + 128]

    for c in inputs[8:]:
        c.wait()
    wf_ref[...] = wm_ref[...].astype(F32)
    for e in range(32):
        wec_ref[32 * e : 32 * e + 32, :] = wf_ref[pl.ds(e, 32, stride=32), :].astype(BF)
    dt_ref[...] = delta_ref[...].astype(F32).reshape(1024, 128).T.astype(BF)
    perm2_ref[...] = ones_where(
        ((rows >> 7) == ((cols >> 4) & 3)) & (((rows >> 4) & 7) == (cols >> 6)) & ((rows & 15) == (cols & 15))
    ).astype(BF)
    product(0)
    spread_right(2)
    product(1)
    product(2)
    product(3)

    for xs in range(4):
        for ys in range(4):
            landed(fall.at[0, 0, 0, 0], fbr.at[xs, ys])
    fcopy = remote(fall.at[core], fall.at[core], fcs.at[0], fcr.at[0], device(core_=other))
    fcopy.start()
    for c in lcopies:
        c.wait_recv()
    for b in range(8):
        for l in range(4):
            for h in range(2):
                left_ref[32 * b + 16 * h : 32 * b + 16 * h + 16, 128 * l : 128 * l + 128] = lall[b // 4, b % 4, 2 * l + h]
    fcopy.wait_recv()

    mi = jnp.concatenate([lall[b // 4, b % 4, 8] for b in range(8)], axis=1)
    mj = jnp.concatenate(
        [jnp.concatenate([fall[g % 2, g // 2, b // 4, b % 4] for b in range(8)], axis=1) for g in range(4)], axis=0
    )
    count = dot(mi, mj, 1, 1).astype(BF)
    lane = iota((64, 512), 1)
    spread = dot(count, ones_where(iota((64, 512), 0) == ((lane >> 7) * 16 + (lane & 15))).astype(BF))
    spread = 1.0 / (spread + 0.001)
    for g in range(4):
        rec_ref[g] = spread[:, 128 * g : 128 * g + 128]

    def scale(i, carry):
        here = pl.ds(pl.multiple_of(i * 32, 32), 32)
        for g in range(4):
            factor = jnp.broadcast_to(rec_ref[g, pl.ds(i, 1), :], (32, 128))
            for l in range(4):
                lanes = slice(256 * l + 128 * (g // 2), 256 * l + 128 * (g // 2) + 128)
                d_ref[g % 2, here, lanes] = (d_ref[g % 2, here, lanes].astype(F32) * factor).astype(BF)
        return carry

    lax.fori_loop(0, 16, scale, 0)

    part = dot(left_ref[...], d_ref[other]).astype(BF)
    for l in range(4):
        for g in range(2):
            lanes = slice(256 * l + 128 * g, 256 * l + 128 * g + 128)
            gsend[:, g, :, 2 * l : 2 * l + 2] = part[:, lanes].reshape(2, 4, 2, 16, 128)
    gcopies = []
    for n in range(2):
        half = rem(tzl + 1 + n, 2)
        c = remote(gsend.at[half], gcore.at[half], gcs.at[n], gcr.at[n], device(core_=other))
        c.start()
        gcopies.append(c)
    part = dot(left_ref[...], d_ref[core])
    for l in range(4):
        for g in range(2):
            lanes = slice(256 * l + 128 * g, 256 * l + 128 * g + 128)
            own_ref[:, g, :, 2 * l : 2 * l + 2] = part[:, lanes].reshape(2, 4, 2, 16, 128)

    gbcopies = []
    for n in range(2):
        half = rem(tzl + 1 + n, 2)
        gcopies[n].wait_recv()
        hsend[half] = (own_ref[half] + gcore[half].astype(F32)).astype(BF)
        for m in range(2):
            x_ = 2 * rem(div(x, 2) + 1 + n, 2) + rem(x + 1 + m, 2)
            hx, _ = twin(x_)
            for dy in (2, 1, 3, 0):
                y_ = rem(y + dy, 4)
                src = hsend.at[half, rem(hx, 2), y_]
                if n == 1 and m == 1 and dy == 0:
                    pltpu.make_async_copy(src, gx.at[x, y], gbr.at[x, y]).start()
                else:
                    c = remote(src, gx.at[x, y], gbs.at[n, m, dy], gbr.at[x, y], device(x_=x_, y_=y_))
                    c.start()
                    gbcopies.append(c)

    ccopies = []
    for n, (dx, dy) in enumerate(NEAR):
        xs, ys = rem(x + dx, 4), rem(y + dy, 4)
        gx_, gzl_ = twin(xs)
        block = rall.at[core, rem(gx_, 2), gzl_, ys]
        landed(block, br.at[xs, ys])
        c = remote(block, block, cs.at[n], cr.at[n], device(core_=other))
        c.start()
        ccopies.append(c)
    for c in ccopies:
        c.wait_recv()

    part = 0.0
    for g in range(2):
        for l in range(4):
            packed = jnp.concatenate(
                [rall[g, h, :, :, 2 * l : 2 * l + 2].reshape(256, 128) for h in range(2)], axis=1
            )
            part = part + dot(packed, d_ref[g, :, 256 * l : 256 * l + 256], 1, 1)
    part = part.astype(BF)
    for b in range(8):
        lsend[b % 4, b // 4] = part[32 * b : 32 * b + 32]
    glcopies = []
    for dy in (2, 1, 3):
        y_ = rem(y + dy, 4)
        c = remote(lsend.at[y_], lrecv.at[dy - 1], gls.at[dy], glr.at[dy], device(y_=y_))
        c.start()
        glcopies.append(c)

    def pair_part(l):
        packed = jnp.concatenate(
            [rall[g % 2, g // 2, :, :, 2 * l : 2 * l + 2].reshape(256, 128) for g in range(4)], axis=1
        )
        right_ref[...] = dot(packed, perm2_ref[...]).astype(BF)
        o = dot(left_ref[...], right_ref[...], 0, 0)
        for t in range(4):
            for p in range(8):
                a, b = swap_halves(
                    o[64 * p : 64 * p + 32, 128 * t : 128 * t + 128],
                    o[64 * p + 32 : 64 * p + 64, 128 * t : 128 * t + 128],
                )
                tile_ref[64 * t : 64 * t + 32, 128 * p : 128 * p + 128] = a
                tile_ref[64 * t + 32 : 64 * t + 64, 128 * p : 128 * p + 128] = b
        term = dot(wt_ref[:, 256 * l : 256 * l + 256], tile_ref[...].astype(BF))
        if l == 0:
            pt_ref[...] = term
        else:
            pt_ref[...] += term


    gzcopies = {}
    for d in (2, 1, 3, 0):
        t = rem(zh + d, 4)
        for s in range(4):
            landed(gx.at[s, t], gbr.at[s, t])
        total = gx[0, t].astype(F32) + gx[1, t].astype(F32) + gx[2, t].astype(F32) + gx[3, t].astype(F32)
        ksend[t] = total.astype(BF)
        c = remote(ksend.at[t], gz.at[zh], gzs.at[d], gzr.at[d], device(x_=tx, zl_=tzl, zh_=t))
        gzcopies[d] = c
        if d:
            c.start()
        else:

            @pl.when(crossed == 1)
            def _():
                c.start()

            @pl.when(crossed == 0)
            def _():
                pltpu.make_async_copy(ksend.at[zh], gz.at[zh], gzr.at[0]).start()

    wt_ref[...] = wec_ref[...].astype(F32).T.astype(BF)
    pair_part(0)
    for c in glcopies:
        c.wait_recv()
    dl = lsend[y].astype(F32) + lrecv[0].astype(F32) + lrecv[1].astype(F32) + lrecv[2].astype(F32)
    lsum[...] = dl.astype(BF)
    glcross = remote(lsum.at[1 - zl], lother, gls.at[0], glr.at[0], device(zl_=1 - zl))
    glcross.start()
    glcopies.append(glcross)
    pair_part(1)
    pair_part(2)
    pair_part(3)
    count = dot(count, ones_where(iota((64, 128), 0) == (iota((64, 128), 1) & 63)).astype(BF)) + 0.001
    low = iota((1, 128), 1) < 64
    denom = jnp.concatenate(
        [jnp.where(low, count[2 * p : 2 * p + 1], count[2 * p + 1 : 2 * p + 2]) for p in range(8)], axis=1
    )
    pair_ref[...] = (pt_ref[...] / denom).T.astype(BF).reshape(16, 64, 128)

    glcross.wait_recv()
    dl = (lsum[zl].astype(F32) + lother[...].astype(F32)) * mask1_ref[...]
    hi, lo = split(jnp.concatenate([dl[:, 32 * i : 32 * i + 32] for i in range(16)], axis=0))
    dnl_ref[...] = dot(hi, w1_ref[...]) + dot(lo, w1_ref[...])

    for d in (0, 1, 3, 2):
        t = rem(zh + 4 - d, 4)
        landed(gz.at[t], gzr.at[d])
    total = gz[0].astype(F32) + gz[1].astype(F32) + gz[2].astype(F32) + gz[3].astype(F32)
    dr = jnp.concatenate(
        [jnp.concatenate([total[2 * l], total[2 * l + 1]], axis=0) for l in range(4)], axis=1
    ) * mask2_ref[...]
    hi, lo = split(dr)
    dr = dot(hi, perm1_ref[...], 1, 1) + dot(lo, perm1_ref[...], 1, 1)

    hi, lo = split(jnp.concatenate([dr[:, 32 * i : 32 * i + 32] for i in range(16)], axis=0))
    dn = dnl_ref[...] + dot(hi, w2_ref[...]) + dot(lo, w2_ref[...])
    for i in range(16):
        for h in range(2):
            dn_ref[h, pl.ds(i, 32, stride=16), :] = dn[32 * i : 32 * i + 32, 128 * h : 128 * h + 128]
    dn = jnp.concatenate([dn_ref[0], dn_ref[1]], axis=1) * gain_ref[...]
    xhat = xhat_ref[...]
    dx = rstd_ref[:, 0:1] * (
        dn - jnp.mean(dn, axis=-1, keepdims=True) - xhat * jnp.mean(dn * xhat, axis=-1, keepdims=True)
    )
    grad_ref[...] = dx.astype(BF).reshape(32, 16, 256)

    for c in [fcopy] + lcopies + ccopies + gcopies + glcopies + gbcopies:
        c.wait_send()
    for d in (1, 2, 3):
        fzcopies[d].wait_send()
        zcopies[d].wait_send()
        gzcopies[d].wait_send()

    @pl.when(crossed == 1)
    def _():
        fzcopies[0].wait_send()
        zcopies[0].wait_send()
        gzcopies[0].wait_send()

    for d in range(4):
        for c in fbcopies[d][:3] + bcopies[d][:3]:
            c.wait_send()

        @pl.when(rem(zh + 4 - d, 4) != y)
        def _():
            fbcopies[d][3].wait_send()
            bcopies[d][3].wait_send()


def body(
    homolog_stack,
    presence_flags,
    normalizer_scaling,
    normalizer_offset,
    first_factor_matrix,
    first_factor_offset,
    second_factor_matrix,
    second_factor_offset,
    final_mapping_matrix,
    coupling_delta_cotangent,
):
    dma = pltpu.SemaphoreType.DMA
    vm = pltpu.VMEM
    whole = pl.BlockSpec(memory_space=pltpu.VMEM)
    far = pl.BlockSpec(memory_space=pltpu.HBM)
    return tuple(
        pl.pallas_call(
            kernel,
            out_shape=(
                vm((16, 64, 128), BF),
                vm((32, 16, 256), BF),
            ),
            in_specs=[far] * 10,
            out_specs=(whole, whole),
            scratch_shapes=[
                vm((32, 16, 256), BF),
                vm((16, 32), jnp.int32),
                vm((1, 256), F32),
                vm((1, 256), F32),
                vm((32, 256), BF),
                vm((1, 32), F32),
                vm((32, 256), BF),
                vm((1, 32), F32),
                vm((1024, 128), BF),
                vm((16, 64, 128), BF),
                dma((10,)),
                vm((512, 256), F32),
                vm((512, 128), F32),
                vm((512, 128), F32),
                vm((1024, 128), F32),
                vm((1024, 128), BF),
                vm((128, 1024), BF),
                vm((128, 1024), BF),
                vm((32, 512), F32),
                vm((32, 512), F32),
                vm((512, 512), BF),
                vm((512, 512), BF),
                vm((16, 128), BF),
                vm((4, 16, 128), BF),
                vm((2, 2, 2, 4, 16, 128), BF),
                vm((8, 16, 128), BF),
                vm((4, 8, 16, 128), BF),
                vm((2, 4, 9, 16, 128), BF),
                vm((2, 2, 2, 4, 8, 16, 128), BF),
                vm((256, 512), BF),
                vm((256, 512), BF),
                vm((256, 1024), F32),
                vm((512, 512), BF),
                vm((2, 512, 1024), BF),
                vm((4, 16, 128), F32),
                vm((128, 1024), F32),
                vm((2, 2, 4, 8, 16, 128), F32),
                vm((2, 2, 4, 8, 16, 128), BF),
                vm((2, 2, 4, 8, 16, 128), BF),
                vm((2, 2, 4, 8, 16, 128), BF),
                vm((4, 4, 8, 16, 128), BF),
                vm((4, 8, 16, 128), BF),
                vm((4, 8, 16, 128), BF),
                vm((4, 2, 32, 512), BF),
                vm((3, 2, 32, 512), BF),
                vm((2, 32, 512), BF),
                vm((32, 512), BF),
                vm((512, 256), F32),
                vm((2, 512, 128), F32),
                dma((4,)), dma((4,)),
                dma((4, 4)), dma((4, 4)),
                dma((1,)), dma((1,)),
                dma((4,)), dma((4,)),
                dma((4, 4)), dma((4, 4)),
                dma((16,)), dma((16,)),
                dma((7,)), dma((7,)),
                dma((2,)), dma((2,)),
                dma((2, 2, 4)), dma((4, 4)),
                dma((4,)), dma((4,)),
                dma((4,)), dma((4,)),
            ],
            compiler_params=pltpu.CompilerParams(
                collective_id=0, has_side_effects=True, vmem_limit_bytes=48 * 1024 * 1024
            ),
        )(
            *(
                pltpu.with_memory_space_constraint(a, pltpu.HBM)
                for a in (
                    homolog_stack,
                    presence_flags.T,
                    normalizer_scaling.reshape(1, 256),
                    normalizer_offset.reshape(1, 256),
                    first_factor_matrix.T,
                    first_factor_offset.reshape(1, 32),
                    second_factor_matrix.T,
                    second_factor_offset.reshape(1, 32),
                    final_mapping_matrix,
                    coupling_delta_cotangent,
                )
            )
        )
    )


def solution(mesh):
    return jax.shard_map(
        body,
        mesh=mesh,
        in_specs=(
            P("seq", "res", None),
            P("seq", "res"),
            P(),
            P(),
            P(),
            P(),
            P(),
            P(),
            P(),
            P("res", "seq", None),
        ),
        out_specs=(P("res", "seq", None), P("seq", "res", None)),
        check_vma=False,
    )
```

```python
import jax
import jax.numpy as jnp
from jax import lax
from jax.experimental import pallas as pl
from jax.experimental.pallas import tpu as pltpu
from jax.sharding import PartitionSpec as P

F32 = jnp.float32
BF = jnp.bfloat16
MESH = pl.DeviceIdType.MESH


def dot(a, b, ca=1, cb=0):
    return lax.dot_general(a, b, (((ca,), (cb,)), ((), ())), preferred_element_type=F32)


def rem(a, n):
    return lax.rem(a, jnp.int32(n))


def div(a, n):
    return lax.div(a, jnp.int32(n))


def split(a):
    hi = a.astype(BF)
    return hi, (a - hi.astype(F32)).astype(BF)


def ones_where(condition):
    return jnp.where(condition, 1.0, 0.0)


def iota(shape, dim):
    return lax.broadcasted_iota(jnp.int32, shape, dim)


def swap_halves(a, b):
    low = iota(a.shape, 1) < 64
    return (
        jnp.where(low, a, pltpu.roll(b, 64, 1)),
        jnp.where(low, pltpu.roll(a, 64, 1), b),
    )


NEAR = ((0, 0), (0, 1), (0, 3), (1, 0), (3, 0), (1, 1), (1, 3), (3, 1), (3, 3), (0, 2), (2, 0), (1, 2), (3, 2), (2, 1), (2, 3), (2, 2))


def kernel(
    x_hbm, flag_hbm, gain_hbm, shift_hbm, w1_hbm, b1_hbm, w2_hbm, b2_hbm, wm_hbm, delta_hbm,
    pair_ref, grad_ref,
    x_ref, flag_ref, gain_ref, shift_ref, w1_ref, b1_ref, w2_ref, b2_ref, wm_ref, delta_ref, in_sem,
    xhat_ref, rstd_ref, proj_ref, wf_ref, wec_ref, wt_ref, dt_ref, mask1_ref, mask2_ref, perm1_ref, perm2_ref,
    fwire, fz, fall, wire, zbuf, lall, rall, left_ref, right_ref, tile_ref, draw_ref, d_ref, rec_ref, pt_ref,
    own_ref, gsend, gcore, hsend, gx, ksend, gz, lsend, lrecv, lsum, lother, dnl_ref, dn_ref,
    fzs, fzr, fbs, fbr, fcs, fcr, zs, zr, bs, br, cs, cr, ls, lr,
    gcs, gcr, gbs, gbr, gzs, gzr, gls, glr,
):
    q = lax.axis_index("seq")
    r = lax.axis_index("res")
    y, zl = div(q, 2), rem(q, 2)
    zh, x, core = div(r, 8), rem(div(r, 2), 4), rem(r, 2)
    other = 1 - core

    def device(x_=x, y_=y, zh_=zh, zl_=zl, core_=core):
        return {"seq": y_ * 2 + zl_, "res": zh_ * 8 + x_ * 2 + core_}

    def twin(x_):
        m = rem(div(x_, 2) + zl, 2)
        return x_ + m * (3 - 2 * x_), rem(zl + m, 2)

    crossed = rem(div(x, 2) + zl, 2)
    tx, tzl = twin(x)

    def remote(src, dst, send, recv, where):
        return pltpu.make_async_remote_copy(
            src_ref=src, dst_ref=dst, send_sem=send, recv_sem=recv, device_id=where, device_id_type=MESH
        )

    def landed(ref, sem):
        pltpu.make_async_copy(ref, ref, sem).wait()

    barrier = pltpu.get_barrier_semaphore()

    def greet(where):
        pl.semaphore_signal(barrier, inc=1, device_id=where, device_id_type=MESH)

    for d in (2, 1, 3):
        greet(device(x_=tx, zl_=tzl, zh_=rem(zh + d, 4)))

    @pl.when(crossed == 1)
    def _():
        greet(device(x_=tx, zl_=tzl))

    for dx, dy in NEAR[:0:-1]:
        greet(device(x_=rem(x + dx, 4), y_=rem(y + dy, 4)))
    for dy in range(4):
        greet(device(y_=rem(y + dy, 4), zl_=1 - zl))
    greet(device(core_=other))

    inputs = [
        pltpu.make_async_copy(a, b, in_sem.at[n])
        for n, (a, b) in enumerate(
            zip(
                (x_hbm, flag_hbm, gain_hbm, shift_hbm, w1_hbm, b1_hbm, w2_hbm, b2_hbm, wm_hbm, delta_hbm),
                (x_ref, flag_ref, gain_ref, shift_ref, w1_ref, b1_ref, w2_ref, b2_ref, wm_ref, delta_ref),
            )
        )
    ]
    for c in inputs:
        c.start()

    inputs[1].wait()
    flags_t = flag_ref[...].astype(F32).astype(BF)
    flags_tile = jnp.concatenate([flags_t, jnp.zeros((16, 96), BF)], axis=1)
    fwire[...] = flags_tile
    lall[zl, y, 8] = flags_tile

    def over_z(src, buf, send, recv):
        copies = {}
        for d in (2, 1, 3, 0):
            copies[d] = remote(src, buf.at[zh], send.at[d], recv.at[d], device(x_=tx, zl_=tzl, zh_=rem(zh + d, 4)))
        for d in (2, 1, 3):
            copies[d].start()

        @pl.when(crossed == 1)
        def _():
            copies[0].start()

        @pl.when(crossed == 0)
        def _():
            pltpu.make_async_copy(src, buf.at[zh], recv.at[0]).start()

        return copies

    def spread_out(d, buf, zrecv, dst, send, recv):
        t = rem(zh + 4 - d, 4)
        landed(buf.at[t], zrecv.at[d])
        place = dst.at[core, rem(tx, 2), tzl, y]
        copies = []
        for dx in (2, 1, 3, 0):
            c = remote(buf.at[t], place, send.at[d, dx], recv.at[x, y], device(x_=rem(x + dx, 4), y_=t))
            copies.append(c)
            if dx:
                c.start()
            else:

                @pl.when(t == y)
                def _():
                    pltpu.make_async_copy(buf.at[t], place, recv.at[x, y]).start()

                @pl.when(t != y)
                def _():
                    c.start()

        return copies

    rows, cols = iota((512, 512), 0), iota((512, 512), 1)
    perm1 = ones_where(((rows >> 5) == (cols & 15)) & ((rows & 31) == (cols >> 4))).astype(BF)
    perm1_ref[...] = perm1
    for n in (0, 2, 3, 4, 5, 6, 7):
        inputs[n].wait()
    xv = x_ref[...].astype(F32).reshape(512, 256)
    centred = xv - jnp.mean(xv, axis=-1, keepdims=True)
    rstd = lax.rsqrt(jnp.mean(centred * centred, axis=-1, keepdims=True) + 1e-5)
    xhat = centred * rstd
    xhat_ref[...] = xhat
    rstd_ref[...] = jnp.broadcast_to(rstd, (512, 128))
    hi, lo = split(xhat * gain_ref[...] + shift_ref[...])
    w = jnp.concatenate([w1_ref[...], w2_ref[...]], axis=0)
    bias = jnp.concatenate([b1_ref[...], b2_ref[...]], axis=1)
    proj_ref[:, 0:64] = dot(hi, w, 1, 1) + dot(lo, w, 1, 1) + bias

    mask1 = dot(flags_t, ones_where(iota((16, 512), 0) == (iota((16, 512), 1) >> 5)).astype(BF), 0, 0)
    mask2 = dot(flags_t, ones_where(iota((16, 512), 0) == (iota((16, 512), 1) & 15)).astype(BF), 0, 0)
    mask1_ref[...] = mask1
    mask2_ref[...] = mask2
    parts = [proj_ref[pl.ds(i, 32, stride=16), :] for i in range(16)]
    lw = (jnp.concatenate([p[:, 0:32] for p in parts], axis=1) * mask1).astype(BF)
    rw = jnp.concatenate([p[:, 32:64] for p in parts], axis=1).astype(BF)
    rw = (dot(rw, perm1) * mask2).astype(BF)
    for l in range(4):
        for h in range(2):
            lall[zl, y, 2 * l + h] = lw[16 * h : 16 * h + 16, 128 * l : 128 * l + 128]
            wire[2 * l + h] = rw[16 * h : 16 * h + 16, 128 * l : 128 * l + 128]
    pl.semaphore_wait(barrier, 23 + crossed)
    fzcopies = over_z(fwire, fz, fzs, fzr)
    zcopies = over_z(wire, zbuf, zs, zr)
    lcopies = [
        remote(
            lall.at[zl, y], lall.at[zl, y], ls.at[k - 1], lr.at[k - 1],
            device(y_=rem(y + k // 2, 4), zl_=rem(zl + k % 2, 2)),
        )
        for k in (4, 2, 6, 5, 3, 7, 1)
    ]

    for c in lcopies:
        c.start()

    fbcopies, bcopies = {}, {}

    def spread_flags(d):
        fbcopies[d] = spread_out(d, fz, fzr, fall, fbs, fbr)

    def spread_right(d):
        bcopies[d] = spread_out(d, zbuf, zr, rall, bs, br)

    spread_flags(0)
    spread_right(0)
    spread_flags(1)
    spread_flags(3)
    spread_flags(2)
    spread_right(1)
    spread_right(3)

    def product(l):
        tile_ref[...] = dot(wec_ref[256 * l : 256 * l + 256, :], dt_ref[...])

        def spread_pair(p, carry):
            lanes = pl.ds(pl.multiple_of(p * 128, 128), 128)
            for t in range(4):
                a, b = swap_halves(tile_ref[64 * t : 64 * t + 32, lanes], tile_ref[64 * t + 32 : 64 * t + 64, lanes])
                place = slice(128 * t, 128 * t + 128)
                draw_ref[pl.ds(pl.multiple_of(p * 64, 64), 32), place] = a.astype(BF)
                draw_ref[pl.ds(pl.multiple_of(p * 64 + 32, 32), 32), place] = b.astype(BF)
            return carry

        lax.fori_loop(0, 8, spread_pair, 0)
        part = dot(draw_ref[...], perm2_ref[...], 1, 1).astype(BF)
        for g in range(4):
            place = slice(256 * l + 128 * (g // 2), 256 * l + 128 * (g // 2) + 128)
            d_ref[g % 2, :, place] = part[:, 128 * g : 128 * g + 128]

    for c in inputs[8:]:
        c.wait()
    wf_ref[...] = wm_ref[...].astype(F32)
    for e in range(32):
        wec_ref[32 * e : 32 * e + 32, :] = wf_ref[pl.ds(e, 32, stride=32), :].astype(BF)
    dt_ref[...] = delta_ref[...].astype(F32).reshape(1024, 128).T.astype(BF)
    perm2_ref[...] = ones_where(
        ((rows >> 7) == ((cols >> 4) & 3)) & (((rows >> 4) & 7) == (cols >> 6)) & ((rows & 15) == (cols & 15))
    ).astype(BF)
    product(0)
    spread_right(2)
    product(1)
    product(2)
    product(3)

    for xs in range(4):
        for ys in range(4):
            landed(fall.at[0, 0, 0, 0], fbr.at[xs, ys])
    fcopy = remote(fall.at[core], fall.at[core], fcs.at[0], fcr.at[0], device(core_=other))
    fcopy.start()
    for c in lcopies:
        c.wait_recv()
    for b in range(8):
        for l in range(4):
            for h in range(2):
                left_ref[32 * b + 16 * h : 32 * b + 16 * h + 16, 128 * l : 128 * l + 128] = lall[b // 4, b % 4, 2 * l + h]
    fcopy.wait_recv()

    mi = jnp.concatenate([lall[b // 4, b % 4, 8] for b in range(8)], axis=1)
    mj = jnp.concatenate(
        [jnp.concatenate([fall[g % 2, g // 2, b // 4, b % 4] for b in range(8)], axis=1) for g in range(4)], axis=0
    )
    count = dot(mi, mj, 1, 1).astype(BF)
    lane = iota((64, 512), 1)
    spread = dot(count, ones_where(iota((64, 512), 0) == ((lane >> 7) * 16 + (lane & 15))).astype(BF))
    spread = 1.0 / (spread + 0.001)
    for g in range(4):
        rec_ref[g] = spread[:, 128 * g : 128 * g + 128]

    def scale(i, carry):
        here = pl.ds(pl.multiple_of(i * 32, 32), 32)
        for g in range(4):
            factor = jnp.broadcast_to(rec_ref[g, pl.ds(i, 1), :], (32, 128))
            for l in range(4):
                lanes = slice(256 * l + 128 * (g // 2), 256 * l + 128 * (g // 2) + 128)
                d_ref[g % 2, here, lanes] = (d_ref[g % 2, here, lanes].astype(F32) * factor).astype(BF)
        return carry

    lax.fori_loop(0, 16, scale, 0)

    part = dot(left_ref[...], d_ref[other]).astype(BF)
    for l in range(4):
        for g in range(2):
            lanes = slice(256 * l + 128 * g, 256 * l + 128 * g + 128)
            gsend[:, g, :, 2 * l : 2 * l + 2] = part[:, lanes].reshape(2, 4, 2, 16, 128)
    gcopies = []
    for n in range(2):
        half = rem(tzl + 1 + n, 2)
        c = remote(gsend.at[half], gcore.at[half], gcs.at[n], gcr.at[n], device(core_=other))
        c.start()
        gcopies.append(c)
    part = dot(left_ref[...], d_ref[core])
    for l in range(4):
        for g in range(2):
            lanes = slice(256 * l + 128 * g, 256 * l + 128 * g + 128)
            own_ref[:, g, :, 2 * l : 2 * l + 2] = part[:, lanes].reshape(2, 4, 2, 16, 128)

    gbcopies = []
    for n in range(2):
        half = rem(tzl + 1 + n, 2)
        gcopies[n].wait_recv()
        hsend[half] = (own_ref[half] + gcore[half].astype(F32)).astype(BF)
        for m in range(2):
            x_ = 2 * rem(div(x, 2) + 1 + n, 2) + rem(x + n + m, 2)
            hx, _ = twin(x_)
            for dy in (2, 1, 3, 0):
                y_ = rem(y + dy, 4)
                src = hsend.at[half, rem(hx, 2), y_]
                if n == 1 and m == 1 and dy == 0:
                    pltpu.make_async_copy(src, gx.at[x, y], gbr.at[x, y]).start()
                else:
                    c = remote(src, gx.at[x, y], gbs.at[n, m, dy], gbr.at[x, y], device(x_=x_, y_=y_))
                    c.start()
                    gbcopies.append(c)

    ccopies = []
    for n, (dx, dy) in enumerate(NEAR):
        xs, ys = rem(x + dx, 4), rem(y + dy, 4)
        gx_, gzl_ = twin(xs)
        block = rall.at[core, rem(gx_, 2), gzl_, ys]
        landed(block, br.at[xs, ys])
        c = remote(block, block, cs.at[n], cr.at[n], device(core_=other))
        c.start()
        ccopies.append(c)
    for c in ccopies:
        c.wait_recv()

    part = 0.0
    for g in range(2):
        for l in range(4):
            packed = jnp.concatenate(
                [rall[g, h, :, :, 2 * l : 2 * l + 2].reshape(256, 128) for h in range(2)], axis=1
            )
            part = part + dot(packed, d_ref[g, :, 256 * l : 256 * l + 256], 1, 1)
    part = part.astype(BF)
    for b in range(8):
        lsend[b % 4, b // 4] = part[32 * b : 32 * b + 32]
    glcopies = []
    for dy in (2, 1, 3):
        y_ = rem(y + dy, 4)
        c = remote(lsend.at[y_], lrecv.at[dy - 1], gls.at[dy], glr.at[dy], device(y_=y_))
        c.start()
        glcopies.append(c)

    def pair_part(l):
        packed = jnp.concatenate(
            [rall[g % 2, g // 2, :, :, 2 * l : 2 * l + 2].reshape(256, 128) for g in range(4)], axis=1
        )
        right_ref[...] = dot(packed, perm2_ref[...]).astype(BF)
        o = dot(left_ref[...], right_ref[...], 0, 0)
        for t in range(4):
            for p in range(8):
                a, b = swap_halves(
                    o[64 * p : 64 * p + 32, 128 * t : 128 * t + 128],
                    o[64 * p + 32 : 64 * p + 64, 128 * t : 128 * t + 128],
                )
                tile_ref[64 * t : 64 * t + 32, 128 * p : 128 * p + 128] = a
                tile_ref[64 * t + 32 : 64 * t + 64, 128 * p : 128 * p + 128] = b
        term = dot(wt_ref[:, 256 * l : 256 * l + 256], tile_ref[...].astype(BF))
        if l == 0:
            pt_ref[...] = term
        else:
            pt_ref[...] += term


    gzcopies = {}
    for d in (2, 1, 3, 0):
        t = rem(zh + d, 4)
        for s in range(4):
            landed(gx.at[s, t], gbr.at[s, t])
        total = gx[0, t].astype(F32) + gx[1, t].astype(F32) + gx[2, t].astype(F32) + gx[3, t].astype(F32)
        ksend[t] = total.astype(BF)
        c = remote(ksend.at[t], gz.at[zh], gzs.at[d], gzr.at[d], device(x_=tx, zl_=tzl, zh_=t))
        gzcopies[d] = c
        if d:
            c.start()
        else:

            @pl.when(crossed == 1)
            def _():
                c.start()

            @pl.when(crossed == 0)
            def _():
                pltpu.make_async_copy(ksend.at[zh], gz.at[zh], gzr.at[0]).start()

    wt_ref[...] = wec_ref[...].astype(F32).T.astype(BF)
    pair_part(0)
    for c in glcopies:
        c.wait_recv()
    dl = lsend[y].astype(F32) + lrecv[0].astype(F32) + lrecv[1].astype(F32) + lrecv[2].astype(F32)
    lsum[...] = dl.astype(BF)
    glcross = remote(lsum.at[1 - zl], lother, gls.at[0], glr.at[0], device(zl_=1 - zl))
    glcross.start()
    glcopies.append(glcross)
    pair_part(1)
    pair_part(2)
    pair_part(3)
    count = dot(count, ones_where(iota((64, 128), 0) == (iota((64, 128), 1) & 63)).astype(BF)) + 0.001
    low = iota((1, 128), 1) < 64
    denom = jnp.concatenate(
        [jnp.where(low, count[2 * p : 2 * p + 1], count[2 * p + 1 : 2 * p + 2]) for p in range(8)], axis=1
    )
    pair_ref[...] = (pt_ref[...] / denom).T.astype(BF).reshape(16, 64, 128)

    glcross.wait_recv()
    dl = (lsum[zl].astype(F32) + lother[...].astype(F32)) * mask1_ref[...]
    hi, lo = split(jnp.concatenate([dl[:, 32 * i : 32 * i + 32] for i in range(16)], axis=0))
    dnl_ref[...] = dot(hi, w1_ref[...]) + dot(lo, w1_ref[...])

    for d in (0, 1, 3, 2):
        t = rem(zh + 4 - d, 4)
        landed(gz.at[t], gzr.at[d])
    total = gz[0].astype(F32) + gz[1].astype(F32) + gz[2].astype(F32) + gz[3].astype(F32)
    dr = jnp.concatenate(
        [jnp.concatenate([total[2 * l], total[2 * l + 1]], axis=0) for l in range(4)], axis=1
    ) * mask2_ref[...]
    hi, lo = split(dr)
    dr = dot(hi, perm1_ref[...], 1, 1) + dot(lo, perm1_ref[...], 1, 1)

    hi, lo = split(jnp.concatenate([dr[:, 32 * i : 32 * i + 32] for i in range(16)], axis=0))
    dn = dnl_ref[...] + dot(hi, w2_ref[...]) + dot(lo, w2_ref[...])
    for i in range(16):
        for h in range(2):
            dn_ref[h, pl.ds(i, 32, stride=16), :] = dn[32 * i : 32 * i + 32, 128 * h : 128 * h + 128]
    dn = jnp.concatenate([dn_ref[0], dn_ref[1]], axis=1) * gain_ref[...]
    xhat = xhat_ref[...]
    dx = rstd_ref[:, 0:1] * (
        dn - jnp.mean(dn, axis=-1, keepdims=True) - xhat * jnp.mean(dn * xhat, axis=-1, keepdims=True)
    )
    grad_ref[...] = dx.astype(BF).reshape(32, 16, 256)

    for c in [fcopy] + lcopies + ccopies + gcopies + glcopies + gbcopies:
        c.wait_send()
    for d in (1, 2, 3):
        fzcopies[d].wait_send()
        zcopies[d].wait_send()
        gzcopies[d].wait_send()

    @pl.when(crossed == 1)
    def _():
        fzcopies[0].wait_send()
        zcopies[0].wait_send()
        gzcopies[0].wait_send()

    for d in range(4):
        for c in fbcopies[d][:3] + bcopies[d][:3]:
            c.wait_send()

        @pl.when(rem(zh + 4 - d, 4) != y)
        def _():
            fbcopies[d][3].wait_send()
            bcopies[d][3].wait_send()


def body(
    homolog_stack,
    presence_flags,
    normalizer_scaling,
    normalizer_offset,
    first_factor_matrix,
    first_factor_offset,
    second_factor_matrix,
    second_factor_offset,
    final_mapping_matrix,
    coupling_delta_cotangent,
):
    dma = pltpu.SemaphoreType.DMA
    vm = pltpu.VMEM
    whole = pl.BlockSpec(memory_space=pltpu.VMEM)
    far = pl.BlockSpec(memory_space=pltpu.HBM)
    return tuple(
        pl.pallas_call(
            kernel,
            out_shape=(
                vm((16, 64, 128), BF),
                vm((32, 16, 256), BF),
            ),
            in_specs=[far] * 10,
            out_specs=(whole, whole),
            scratch_shapes=[
                vm((32, 16, 256), BF),
                vm((16, 32), jnp.int32),
                vm((1, 256), F32),
                vm((1, 256), F32),
                vm((32, 256), BF),
                vm((1, 32), F32),
                vm((32, 256), BF),
                vm((1, 32), F32),
                vm((1024, 128), BF),
                vm((16, 64, 128), BF),
                dma((10,)),
                vm((512, 256), F32),
                vm((512, 128), F32),
                vm((512, 128), F32),
                vm((1024, 128), F32),
                vm((1024, 128), BF),
                vm((128, 1024), BF),
                vm((128, 1024), BF),
                vm((32, 512), F32),
                vm((32, 512), F32),
                vm((512, 512), BF),
                vm((512, 512), BF),
                vm((16, 128), BF),
                vm((4, 16, 128), BF),
                vm((2, 2, 2, 4, 16, 128), BF),
                vm((8, 16, 128), BF),
                vm((4, 8, 16, 128), BF),
                vm((2, 4, 9, 16, 128), BF),
                vm((2, 2, 2, 4, 8, 16, 128), BF),
                vm((256, 512), BF),
                vm((256, 512), BF),
                vm((256, 1024), F32),
                vm((512, 512), BF),
                vm((2, 512, 1024), BF),
                vm((4, 16, 128), F32),
                vm((128, 1024), F32),
                vm((2, 2, 4, 8, 16, 128), F32),
                vm((2, 2, 4, 8, 16, 128), BF),
                vm((2, 2, 4, 8, 16, 128), BF),
                vm((2, 2, 4, 8, 16, 128), BF),
                vm((4, 4, 8, 16, 128), BF),
                vm((4, 8, 16, 128), BF),
                vm((4, 8, 16, 128), BF),
                vm((4, 2, 32, 512), BF),
                vm((3, 2, 32, 512), BF),
                vm((2, 32, 512), BF),
                vm((32, 512), BF),
                vm((512, 256), F32),
                vm((2, 512, 128), F32),
                dma((4,)), dma((4,)),
                dma((4, 4)), dma((4, 4)),
                dma((1,)), dma((1,)),
                dma((4,)), dma((4,)),
                dma((4, 4)), dma((4, 4)),
                dma((16,)), dma((16,)),
                dma((7,)), dma((7,)),
                dma((2,)), dma((2,)),
                dma((2, 2, 4)), dma((4, 4)),
                dma((4,)), dma((4,)),
                dma((4,)), dma((4,)),
            ],
            compiler_params=pltpu.CompilerParams(
                collective_id=0, has_side_effects=True, vmem_limit_bytes=48 * 1024 * 1024
            ),
        )(
            *(
                pltpu.with_memory_space_constraint(a, pltpu.HBM)
                for a in (
                    homolog_stack,
                    presence_flags.T,
                    normalizer_scaling.reshape(1, 256),
                    normalizer_offset.reshape(1, 256),
                    first_factor_matrix.T,
                    first_factor_offset.reshape(1, 32),
                    second_factor_matrix.T,
                    second_factor_offset.reshape(1, 32),
                    final_mapping_matrix,
                    coupling_delta_cotangent,
                )
            )
        )
    )


def solution(mesh):
    return jax.shard_map(
        body,
        mesh=mesh,
        in_specs=(
            P("seq", "res", None),
            P("seq", "res"),
            P(),
            P(),
            P(),
            P(),
            P(),
            P(),
            P(),
            P("res", "seq", None),
        ),
        out_specs=(P("res", "seq", None), P("seq", "res", None)),
        check_vma=False,
    )
```
